32 devices in a mesh: dp: 8 (over z, y), blk: 4 (over x, core).
Axes of the slice: x: 2, y: 2, z: 4, core: 2. Of those that a mesh axis runs over, the one named last changes fastest.
Arguments:
- grad_partial: bfloat16 [8, 8, 1024, 1024], P('dp', 'blk'), may hold values from -1 to 1
- left_stat: float32 [8, 1024, 1024], P('blk', 'dp'), may hold values from -0.5 to 10, as said below
- right_stat: float32 [8, 1024, 1024], P('blk', 'dp'), may hold values from -0.5 to 10, as said below
- left_root: bfloat16 [8, 1024, 1024], P('blk', 'dp'), may hold values from -0.2 to 2, as said below
- right_root: bfloat16 [8, 1024, 1024], P('blk', 'dp'), may hold values from -0.2 to 2, as said below
- second_moment: float32 [8, 1024, 1024], P('blk', 'dp'), may hold values from 0.0003 to 0.01
Outputs:
- update: bfloat16 [8, 1024, 1024], P('blk')
- left_new: float32 [8, 1024, 1024], P('blk', 'dp')
- right_new: float32 [8, 1024, 1024], P('blk', 'dp')
- moment_new: float32 [8, 1024, 1024], P('blk', 'dp')
The draws below stay inside these ranges and needn't reach their ends.
Inputs may be any that keep to these rules, and one draw needn't show every extreme that they name: `left_stat`: each block is symmetric. `right_stat`: each block is symmetric. `left_root`: each block is symmetric. `right_root`: each block is symmetric.
All inputs are finite; a program needn't handle non-finite values.
Results may differ from the reference program's by a relative error of at most 0.027.
Values may be sent and summed in bfloat16 or wider, within the bound.
No kernel may reach another device: no remote copies, remote signals or barrier semaphores. Data moves between devices by JAX's collectives and lax.ppermute only.
A program may use at most 128 MiB of HBM per device.

```python
import math
import jax
import jax.numpy as jnp
from jax import lax

B = 1024
NB = 8
REPLICAS = 8


def dominant(base_key, lowest, highest, spread, limit):
    key_diag, key_off = jax.random.split(base_key)
    diagonal = jnp.exp(jax.random.uniform(key_diag, (NB, B, 1), jnp.float32, math.log(lowest), math.log(highest)))
    random_part = jax.random.normal(key_off, (NB, B, B), jnp.float32)
    symmetric = (random_part + jnp.swapaxes(random_part, 1, 2)) * (spread / math.sqrt(2.0 * B))
    symmetric = jnp.clip(symmetric, -limit, limit)
    identity = (lax.broadcasted_iota(jnp.int32, (B, B), 0) == lax.broadcasted_iota(jnp.int32, (B, B), 1)).astype(jnp.float32)
    return symmetric * (1.0 - identity) + diagonal * identity


def draw_grad_partial(key, part):
    key = jax.random.fold_in(key, 1)
    key_row, key_own = jax.random.split(key, 2)
    row_pos = lax.broadcasted_iota(jnp.float32, (NB, B, 1), 1) / B
    block_pos = lax.broadcasted_iota(jnp.float32, (NB, B, 1), 0) / NB
    jitter = jax.random.uniform(key_row, (NB, B, 1), jnp.float32)
    row_scale = 0.03 * 10.0 ** (0.5 * row_pos + 0.2 * block_pos + 0.5 * jitter)
    blended = jax.random.normal(key_own, (REPLICAS, NB, B, B), jnp.float32) / math.sqrt(REPLICAS)
    return (blended * row_scale).astype(jnp.bfloat16)


def draw_left_stat(key, part):
    key = jax.random.fold_in(key, 2)
    return dominant(key, 1.0, 10.0, 1.0, 0.48)


def draw_right_stat(key, part):
    key = jax.random.fold_in(key, 3)
    return dominant(key, 1.0, 10.0, 1.0, 0.48)


def draw_left_root(key, part):
    key = jax.random.fold_in(key, 4)
    return dominant(key, 0.5, 2.0, 0.4, 0.19).astype(jnp.bfloat16)


def draw_right_root(key, part):
    key = jax.random.fold_in(key, 5)
    return dominant(key, 0.5, 2.0, 0.4, 0.19).astype(jnp.bfloat16)


def draw_second_moment(key, part):
    key = jax.random.fold_in(key, 6)
    row_pos = lax.broadcasted_iota(jnp.float32, (NB, B, 1), 1) / B
    exponent = jax.random.uniform(key, (NB, B, B), jnp.float32)
    return 0.001 * 10.0 ** (exponent - 0.5 * row_pos)


def setup_inputs(seed: int = 0) -> dict:
    key_list = jax.random.split(jax.random.key(seed), 7)
    return {
        "grad_partial": draw_grad_partial(jax.random.fold_in(key_list[6], 71), 0),
        "left_stat": draw_left_stat(jax.random.fold_in(key_list[6], 71), 0),
        "right_stat": draw_right_stat(jax.random.fold_in(key_list[6], 71), 0),
        "left_root": draw_left_root(jax.random.fold_in(key_list[6], 71), 0),
        "right_root": draw_right_root(jax.random.fold_in(key_list[6], 71), 0),
        "second_moment": draw_second_moment(jax.random.fold_in(key_list[6], 71), 0),
    }


stat_decay = 0.95
moment_decay = 0.999
epsilon = 1e-08

def reference(grad_partial, left_stat, right_stat, left_root, right_root, second_moment):

    def accumulate(running, replica_term):
        return (running + replica_term.astype(jnp.float32), None)
    gradient = lax.scan(accumulate, jnp.zeros((NB, B, B), jnp.float32), grad_partial)[0]
    grad_low = gradient.astype(jnp.bfloat16)
    grad_wide = grad_low.astype(jnp.float32)
    left_new = stat_decay * left_stat + (1.0 - stat_decay) * jnp.einsum('nik,njk->nij', grad_wide, grad_wide)
    right_new = stat_decay * right_stat + (1.0 - stat_decay) * jnp.einsum('nki,nkj->nij', grad_wide, grad_wide)
    mixed_left = jnp.einsum('nik,nkj->nij', left_root.astype(jnp.float32), grad_wide).astype(jnp.bfloat16)
    precond = jnp.einsum('nik,nkj->nij', mixed_left.astype(jnp.float32), right_root.astype(jnp.float32)).astype(jnp.bfloat16)
    moment_new = moment_decay * second_moment + (1.0 - moment_decay) * gradient * gradient
    adam_dir = gradient / (jnp.sqrt(moment_new) + epsilon)
    adam_sq = jnp.sum(adam_dir * adam_dir)
    precond_wide = precond.astype(jnp.float32)
    precond_sq = jnp.sum(precond_wide * precond_wide)
    factor = jnp.sqrt(adam_sq / precond_sq)
    update = (factor * precond_wide).astype(jnp.bfloat16)
    return (update, left_new, right_new, moment_new)
```

```python
import functools

import jax
import jax.numpy as jnp
from jax import lax
from jax.experimental import pallas as pl
from jax.experimental.pallas import tpu as pltpu
from jax.sharding import PartitionSpec as P

stat_decay = 0.95
moment_decay = 0.999
epsilon = 1e-08

f32 = jnp.float32
bf16 = jnp.bfloat16


def bits_of(count):
    bits = count.bit_length() - 1
    assert count == 1 << bits
    return bits


VMEM = pl.BlockSpec(memory_space=pltpu.VMEM)
SMEM = pl.BlockSpec(memory_space=pltpu.SMEM)


def call(kernel, out_shape, name, flops=0):
    def run(place, *arrays):
        size = sum(a.size * a.dtype.itemsize for a in arrays)
        return pl.pallas_call(
            kernel,
            out_shape=out_shape,
            in_specs=[SMEM] + [VMEM] * len(arrays),
            out_specs=jax.tree.map(lambda _: VMEM, out_shape),
            compiler_params=pltpu.CompilerParams(vmem_limit_bytes=24 * 2**20),
            cost_estimate=pl.CostEstimate(flops=flops, bytes_accessed=size, transcendentals=0),
            name=name,
        )(place, *arrays)

    return run


def block_span(members, rows, part, member):
    return pl.ds(pl.multiple_of((part * members + member) * rows, rows), rows)


def cut_kernel(bits, orders, flip, grads_ref, *refs):
    out_refs, sems = refs[:-1], refs[-1]
    index = lax.axis_index("dp")
    copies = []
    for part, (first, out_ref) in enumerate(zip(orders, out_refs)):
        own = (index >> first) & 1
        for i in range(out_ref.shape[0]):
            rest = [(i >> j) & 1 for j in range(bits - 1)]
            rest.insert(first, 1 - own if flip else own)
            member = sum(bit << j for j, bit in enumerate(rest[:-1]))
            source = grads_ref.at[rest[-1], part, member]
            copy = pltpu.make_async_copy(source, out_ref.at[i], sems.at[len(copies)])
            copy.start()
            copies.append(copy)
    for copy in copies:
        copy.wait()


def cut(grads, bits, orders, flip):
    members, rows, width = grads.shape[2:]
    shape = jax.ShapeDtypeStruct((members, rows, width), bf16)
    return pl.pallas_call(
        functools.partial(cut_kernel, bits, orders, flip),
        out_shape=(shape, shape),
        in_specs=[pl.BlockSpec(memory_space=pl.ANY)],
        out_specs=(VMEM, VMEM),
        scratch_shapes=[pltpu.SemaphoreType.DMA((2 * members,))],
        compiler_params=pltpu.CompilerParams(vmem_limit_bytes=(56 if flip else 24) * 2**20),
        cost_estimate=pl.CostEstimate(flops=0, bytes_accessed=8 * members * rows * width, transcendentals=0),
        name="cut",
    )(grads)


def sum_kernel(axes_lists, places, free, place_ref, *refs):
    index, out_ref = place_ref[2], refs[-1]
    for i in range(1 << len(free)):
        total = None
        for axes, ref in zip(axes_lists, refs):
            at = 0
            for axis in axes:
                if axis in places:
                    bit = (index >> axis) & 1
                    at = at * 2 + (1 - bit if places[axis] else bit)
                else:
                    at = at * 2 + ((i >> (len(free) - 1 - free.index(axis))) & 1)
            piece = ref[at].astype(f32)
            total = piece if total is None else total + piece
        out_ref[i] = total.astype(bf16)


def sum_pieces(place, terms, places):
    arrays = [array.reshape((-1,) + array.shape[-2:]) for array, _ in terms]
    axes_lists = [axes for _, axes in terms]
    free = [axis for axis in axes_lists[0] if axis not in places]
    shape = arrays[0].shape[-2:]
    kernel = functools.partial(sum_kernel, axes_lists, places, free)
    out = call(kernel, jax.ShapeDtypeStruct((1 << len(free),) + shape, bf16), "sum_pieces")(place, *arrays)
    return out.reshape([2] * len(free) + list(shape))


def neighbour_of(member):
    return member ^ (1 + ((member ^ (member >> 1)) & 1))


def pack_kernel(members, rows, place_ref, own_ref, partner_ref, pair_ref, message_ref):
    member, half = place_ref[0], place_ref[1]
    pair_ref[half] = own_ref[half]
    pair_ref[1 - half] = partner_ref[...]
    role = member >> 1
    blocks = [(0, 0, member), (0, 1, member), (1, 1, member)]
    blocks += [(row_part, part, neighbour_of(member)) for row_part in range(2) for part in range(2)]
    blocks += [(0, role, member ^ 3), (role, 1, member ^ 3)]
    for i, (row_part, part, column) in enumerate(blocks):
        message_ref[i] = pair_ref[row_part, :, block_span(members, rows, part, column)]


def pack(place, own, partner, members):
    rows, width = own.shape[1:]
    out_shape = (jax.ShapeDtypeStruct((2, rows, width), bf16), jax.ShapeDtypeStruct((9, rows, rows), bf16))
    return call(functools.partial(pack_kernel, members, rows), out_shape, "pack")(place, own, partner)


def unfold_kernel(members, rows, place_ref, pair_ref, *refs):
    message_refs, whole_ref = refs[:-1], refs[-1]
    member = place_ref[0]

    def put(row_part, row_member, part, column_member, block):
        whole_ref[
            block_span(members, rows, row_part, row_member), block_span(members, rows, part, column_member)
        ] = block

    for row_part in range(2):
        whole_ref[block_span(members, rows, row_part, member), :] = pair_ref[row_part]
    for k, message_ref in enumerate(message_refs, 1):
        sender = member ^ k
        neighbour, opposite, role = neighbour_of(sender), sender ^ 3, sender >> 1
        for row_part in range(2):
            for part in range(2):
                mine = pair_ref[row_part, :, block_span(members, rows, part, sender)]
                put(part, sender, row_part, member, mine.T)
                block = message_ref[3 + 2 * row_part + part]
                put(row_part, sender, part, neighbour, block)
                put(part, neighbour, row_part, sender, block.T)
        put(0, sender, 0, sender, message_ref[0])
        put(0, sender, 1, sender, message_ref[1])
        put(1, sender, 0, sender, message_ref[1].T)
        put(1, sender, 1, sender, message_ref[2])
        put(0, sender, role, opposite, message_ref[7])
        put(role, opposite, 0, sender, message_ref[7].T)
        put(role, sender, 1, opposite, message_ref[8])
        put(1, opposite, role, sender, message_ref[8].T)


def unfold(place, pair, messages, members):
    rows, width = pair.shape[1:]
    out_shape = jax.ShapeDtypeStruct((2 * members * rows, width), bf16)
    return call(functools.partial(unfold_kernel, members, rows), out_shape, "unfold")(place, pair, *messages)


def place_kernel(members, rows, place_ref, *refs):
    for k in range(members):
        for part in range(2):
            refs[-1][block_span(members, rows, part, place_ref[0] ^ k), :] = refs[k][part]


def place_rows(place, pieces):
    members = len(pieces)
    rows, width = pieces[0].shape[1:]
    out_shape = jax.ShapeDtypeStruct((2 * members * rows, width), bf16)
    return call(functools.partial(place_kernel, members, rows), out_shape, "place_rows")(place, *pieces)


def two_products(left, grad_ref, right_ref):
    mixed_left = jnp.dot(left, grad_ref[...], preferred_element_type=f32).astype(bf16)
    return jnp.dot(mixed_left, right_ref[...], preferred_element_type=f32).astype(bf16)


def product_kernel(members, rows, place_ref, *refs):
    grad_pieces = refs[: 2 * members]
    right_ref, left_ref, precond_ref, grad_ref, square_ref = refs[2 * members :]
    for part in range(2):
        for k in range(members):
            grad_ref[block_span(members, rows, part, place_ref[0] ^ k), :] = grad_pieces[part * members + k][...]
    precond = two_products(left_ref[...], grad_ref, right_ref)
    precond_ref[...] = precond
    precond_wide = precond.astype(f32)
    square_ref[...] = jnp.full(square_ref.shape, jnp.sum(precond_wide * precond_wide))


def product(place, grad_pieces, right_full, left_pair):
    members = len(grad_pieces) // 2
    rows, width = grad_pieces[0].shape
    out_shape = (
        jax.ShapeDtypeStruct((2 * rows, width), bf16),
        jax.ShapeDtypeStruct((2 * rows * members, width), bf16),
        jax.ShapeDtypeStruct((8, 128), f32),
    )
    kernel = functools.partial(product_kernel, members, rows)
    return call(kernel, out_shape, "product", 8 * rows * width * width)(place, *grad_pieces, right_full, left_pair)


def per_device(devices, groups, grad_partial, left_stat, right_stat, left_root, right_root, second_moment):
    bits = bits_of(devices)
    top = bits - 1
    members = devices // 2
    index = lax.axis_index("dp")
    member, half = index % members, index // members
    rows, width = left_stat.shape[1:]

    def swap(array, bit):
        return lax.ppermute(array, "dp", [(i, i ^ (1 << bit)) for i in range(devices)])

    def after(array, *arrays):
        return lax.optimization_barrier((array, *arrays))[0]

    def gather_pieces(own, *before_forward):
        pieces = {0: own}
        for bit in range(top - 1, -1, -1):
            for k in list(pieces):
                source = after(pieces[k], *before_forward) if k and before_forward else pieces[k]
                pieces[k ^ (1 << bit)] = swap(source, bit)
        return pieces

    def gather_direct(own):
        pieces = {0: own}
        for k in range(members - 1, 0, -1):
            pieces[k] = lax.ppermute(own, "dp", [(i, i ^ k) for i in range(devices)])
        return pieces

    def by_half(own, partner):
        return jnp.stack([jnp.where(half == 0, own, partner), jnp.where(half == 0, partner, own)])

    def choose(stack, place):
        return lax.dynamic_index_in_dim(stack, place, 0, keepdims=False)

    member_axes = list(range(top - 1, -1, -1))
    grads = grad_partial[0].reshape(2, 2, members, rows, width)
    lower = list(range(top))
    orders = (lower + [top], lower[::-1] + [top])
    first_sends = cut(grads, bits, [order[0] for order in orders], True)
    first_own = cut(after(grads, *first_sends), bits, [order[0] for order in orders], False)
    terms, places = [[], []], [{}, {}]
    right_partner = swap(choose(right_root, 1 - half), top)

    place = jnp.stack([member, half, index])

    def reduce_step(part, step, *arrays):
        bit = orders[part][step]
        if step == 0:
            send = first_sends[part]
        else:
            if arrays:
                array, axes = terms[part][-1]
                terms[part][-1] = (after(array, *arrays), axes)
            send = sum_pieces(place, terms[part], {**places[part], bit: True})
        places[part][bit] = False
        axes = [b for b in [top] + member_axes if b not in places[part]]
        if step == 0:
            terms[part] = [(first_own[part], axes)]
        terms[part].append((swap(send, bit), axes))
        return send

    def reduced(part):
        return sum_pieces(place, terms[part], places[part])

    reduce_step(1, 0)
    reduce_step(0, 0)
    left_partner = swap(after(choose(left_root, 1 - half), terms[0][-1][0], terms[1][-1][0]), top)
    for step in range(1, bits - 1):
        for part in range(2):
            reduce_step(part, step, right_partner)
    round_ends = [t[-1][0] for t in terms]

    halved = members == 4 and rows % 128 == 0

    def pair_rows(own, partner):
        if halved:
            return pack(place, own, partner, members)
        pair = by_half(choose(own, half), partner)
        return pair, pair

    def whole_matrix(pair, pieces):
        if halved:
            return unfold(place, pair, [pieces[k] for k in range(1, members)], members)
        return place_rows(place, [pieces[k] for k in range(members)])

    def exchanged(pieces):
        return [pieces[1 << bit] for bit in member_axes]

    last_send = reduce_step(0, bits - 1, *round_ends, left_partner)
    right_pair, right_message = pair_rows(right_root, right_partner)
    right_pieces = gather_pieces(after(right_message, last_send))
    low = [reduced(0)]
    reduce_step(1, bits - 1, low[0])
    grad_pieces = [gather_pieces(after(low[0], *exchanged(right_pieces)))]
    right_full = whole_matrix(right_pair, right_pieces)
    low.append(after(reduced(1), *exchanged(grad_pieces[0])))
    grad_pieces.append(gather_direct(low[1]))
    own_low = jnp.stack(low)
    theirs = swap(choose(own_low, 1 - half), top)

    span = 2 * rows
    left_pair = by_half(choose(left_root, half), left_partner)
    precond, grad_low, precond_part = product(
        place,
        [pieces[k] for pieces in grad_pieces for k in range(members)],
        right_full,
        left_pair.reshape(span, width),
    )
    precond = precond.reshape(2, rows, width)
    theirs, own_low, grad_low = (after(array, precond) for array in (theirs, own_low, grad_low))

    first_pieces = {0: precond}
    for bit in range(top - 1, 0, -1):
        for k in list(first_pieces):
            first_pieces[k ^ (1 << bit)] = swap(first_pieces[k], bit)
    first_pieces[1] = swap(precond, 0)
    partner = swap(precond, top)

    grad_rows = by_half(choose(own_low, half), theirs).astype(f32)
    moment_new = moment_decay * second_moment + (1.0 - moment_decay) * grad_rows * grad_rows
    adam_dir = grad_rows / (jnp.sqrt(moment_new) + epsilon)
    adam_part = jnp.sum(adam_dir * adam_dir)

    lane = lax.broadcasted_iota(jnp.int32, (8, 128), 1)
    sums = jnp.where(lane == 0, adam_part, precond_part)
    for bit in range(bits_of(groups)):
        sums = sums + lax.ppermute(sums, "blk", [(i, i ^ (1 << bit)) for i in range(groups)])
    for bit in range(bits):
        if bit == top:
            sums = after(sums, partner, *first_pieces.values())
        sums = sums + swap(sums, bit)

    def columns(part):
        return lax.dynamic_slice_in_dim(grad_low, part * members * rows + member * rows, rows, 1)

    contract_rows = (((0,), (0,)), ((), ()))
    contract_cols = (((1,), (1,)), ((), ()))
    right_gram = [lax.dot_general(columns(p), grad_low, contract_rows, preferred_element_type=f32) for p in range(2)]
    right_gram = jnp.stack(right_gram)
    left_gram = lax.dot_general(own_low.reshape(span, width), grad_low, contract_cols, preferred_element_type=f32)
    left_gram = left_gram.reshape(2, rows, width)
    left_away = choose(left_gram, 1 - half).astype(bf16)
    right_away = choose(right_gram, 1 - half).astype(bf16)

    partner, *arrived = lax.optimization_barrier((partner, *first_pieces.values()))
    first_pieces = dict(zip(first_pieces, arrived))
    onward = [k for k in first_pieces if k > 1]
    neighbour = swap(jnp.stack([first_pieces[k] for k in onward] + [partner]), 0)
    for i, k in enumerate(onward):
        first_pieces[k ^ 1] = neighbour[i]
    second_pieces = {0: partner, 1: neighbour[-1]}
    for k in range(members - 1, 1, -1):
        second_pieces[k] = lax.ppermute(partner, "dp", [(i, i ^ k) for i in range(devices)])
    grams_away = after(jnp.stack([left_away, right_away]), partner)
    grams_partner = swap(grams_away, top)

    factor = jnp.sqrt(sums[0, 0] / sums[0, 1])
    update = jnp.zeros((2, 2, members, rows, width), bf16)
    for block, pieces in ((half, first_pieces), (1 - half, second_pieces)):
        for k, piece in pieces.items():
            scaled = (factor * piece.astype(f32)).astype(bf16)
            update = lax.dynamic_update_slice(update, scaled[None, :, None], (block, 0, member ^ k, 0, 0))
    update = update.reshape(2, width, width)
    left_partner, right_partner = after(grams_partner, update)

    def new_stat(stat, gram, partner):
        return stat_decay * stat + (1.0 - stat_decay) * by_half(choose(gram, half), partner.astype(f32))

    left_new = new_stat(left_stat, left_gram, left_partner)
    right_new = new_stat(right_stat, right_gram, right_partner)
    return (update, left_new, right_new, moment_new)


def solution(mesh):
    in_specs = (
        P("dp", "blk", None, None),
        P("blk", "dp", None),
        P("blk", "dp", None),
        P("blk", "dp", None),
        P("blk", "dp", None),
        P("blk", "dp", None),
    )
    out_specs = (
        P("blk", None, None),
        P("blk", "dp", None),
        P("blk", "dp", None),
        P("blk", "dp", None),
    )

    def body(*arrays):
        return per_device(mesh.shape["dp"], mesh.shape["blk"], *arrays)

    return jax.shard_map(body, mesh=mesh, in_specs=in_specs, out_specs=out_specs, check_vma=False)
```

```python
import functools

import jax
import jax.numpy as jnp
from jax import lax
from jax.experimental import pallas as pl
from jax.experimental.pallas import tpu as pltpu
from jax.sharding import PartitionSpec as P

stat_decay = 0.95
moment_decay = 0.999
epsilon = 1e-08

f32 = jnp.float32
bf16 = jnp.bfloat16


def bits_of(count):
    bits = count.bit_length() - 1
    assert count == 1 << bits
    return bits


VMEM = pl.BlockSpec(memory_space=pltpu.VMEM)
SMEM = pl.BlockSpec(memory_space=pltpu.SMEM)


def call(kernel, out_shape, name, flops=0):
    def run(place, *arrays):
        size = sum(a.size * a.dtype.itemsize for a in arrays)
        return pl.pallas_call(
            kernel,
            out_shape=out_shape,
            in_specs=[SMEM] + [VMEM] * len(arrays),
            out_specs=jax.tree.map(lambda _: VMEM, out_shape),
            compiler_params=pltpu.CompilerParams(vmem_limit_bytes=24 * 2**20),
            cost_estimate=pl.CostEstimate(flops=flops, bytes_accessed=size, transcendentals=0),
            name=name,
        )(place, *arrays)

    return run


def block_span(members, rows, part, member):
    return pl.ds(pl.multiple_of((part * members + member) * rows, rows), rows)


def cut_kernel(bits, orders, flip, grads_ref, *refs):
    out_refs, sems = refs[:-1], refs[-1]
    index = lax.axis_index("dp")
    copies = []
    for part, (first, out_ref) in enumerate(zip(orders, out_refs)):
        own = (index >> first) & 1
        for i in range(out_ref.shape[0]):
            rest = [(i >> j) & 1 for j in range(bits - 1)]
            rest.insert(first, 1 - own if flip else own)
            member = sum(bit << j for j, bit in enumerate(rest[:-1]))
            source = grads_ref.at[rest[-1], part, member]
            copy = pltpu.make_async_copy(source, out_ref.at[i], sems.at[len(copies)])
            copy.start()
            copies.append(copy)
    for copy in copies:
        copy.wait()


def cut(grads, bits, orders, flip):
    members, rows, width = grads.shape[2:]
    shape = jax.ShapeDtypeStruct((members, rows, width), bf16)
    return pl.pallas_call(
        functools.partial(cut_kernel, bits, orders, flip),
        out_shape=(shape, shape),
        in_specs=[pl.BlockSpec(memory_space=pl.ANY)],
        out_specs=(VMEM, VMEM),
        scratch_shapes=[pltpu.SemaphoreType.DMA((2 * members,))],
        compiler_params=pltpu.CompilerParams(vmem_limit_bytes=(56 if flip else 24) * 2**20),
        cost_estimate=pl.CostEstimate(flops=0, bytes_accessed=8 * members * rows * width, transcendentals=0),
        name="cut",
    )(grads)


def sum_kernel(axes_lists, places, free, place_ref, *refs):
    index, out_ref = place_ref[2], refs[-1]
    for i in range(1 << len(free)):
        total = None
        for axes, ref in zip(axes_lists, refs):
            at = 0
            for axis in axes:
                if axis in places:
                    bit = (index >> axis) & 1
                    at = at * 2 + (1 - bit if places[axis] else bit)
                else:
                    at = at * 2 + ((i >> (len(free) - 1 - free.index(axis))) & 1)
            piece = ref[at].astype(f32)
            total = piece if total is None else total + piece
        out_ref[i] = total.astype(bf16)


def sum_pieces(place, terms, places):
    arrays = [array.reshape((-1,) + array.shape[-2:]) for array, _ in terms]
    axes_lists = [axes for _, axes in terms]
    free = [axis for axis in axes_lists[0] if axis not in places]
    shape = arrays[0].shape[-2:]
    kernel = functools.partial(sum_kernel, axes_lists, places, free)
    out = call(kernel, jax.ShapeDtypeStruct((1 << len(free),) + shape, bf16), "sum_pieces")(place, *arrays)
    return out.reshape([2] * len(free) + list(shape))


def neighbour_of(member):
    return member ^ (1 + ((member ^ (member >> 1)) & 1))


def pack_kernel(members, rows, place_ref, own_ref, partner_ref, pair_ref, message_ref):
    member, half = place_ref[0], place_ref[1]
    pair_ref[half] = own_ref[half]
    pair_ref[1 - half] = partner_ref[...]
    role = member >> 1
    blocks = [(0, 0, member), (0, 1, member), (1, 1, member)]
    blocks += [(row_part, part, neighbour_of(member)) for row_part in range(2) for part in range(2)]
    blocks += [(0, role, member ^ 3), (role, 1, member ^ 3)]
    for i, (row_part, part, column) in enumerate(blocks):
        message_ref[i] = pair_ref[row_part, :, block_span(members, rows, part, column)]


def pack(place, own, partner, members):
    rows, width = own.shape[1:]
    out_shape = (jax.ShapeDtypeStruct((2, rows, width), bf16), jax.ShapeDtypeStruct((9, rows, rows), bf16))
    return call(functools.partial(pack_kernel, members, rows), out_shape, "pack")(place, own, partner)


def unfold_kernel(members, rows, place_ref, pair_ref, *refs):
    message_refs, whole_ref = refs[:-1], refs[-1]
    member = place_ref[0]

    def put(row_part, row_member, part, column_member, block):
        whole_ref[
            block_span(members, rows, row_part, row_member), block_span(members, rows, part, column_member)
        ] = block

    for row_part in range(2):
        whole_ref[block_span(members, rows, row_part, member), :] = pair_ref[row_part]
    for k, message_ref in enumerate(message_refs, 1):
        sender = member ^ k
        neighbour, opposite, role = neighbour_of(sender), sender ^ 3, sender >> 1
        for row_part in range(2):
            for part in range(2):
                mine = pair_ref[row_part, :, block_span(members, rows, part, sender)]
                put(part, sender, row_part, member, mine.T)
                block = message_ref[3 + 2 * row_part + part]
                put(row_part, sender, part, neighbour, block)
                put(part, neighbour, row_part, sender, block.T)
        put(0, sender, 0, sender, message_ref[0])
        put(0, sender, 1, sender, message_ref[1])
        put(1, sender, 0, sender, message_ref[1].T)
        put(1, sender, 1, sender, message_ref[2])
        put(0, sender, role, opposite, message_ref[7])
        put(role, opposite, 0, sender, message_ref[7].T)
        put(role, sender, 1, opposite, message_ref[8])
        put(1, opposite, role, sender, message_ref[8].T)


def unfold(place, pair, messages, members):
    rows, width = pair.shape[1:]
    out_shape = jax.ShapeDtypeStruct((2 * members * rows, width), bf16)
    return call(functools.partial(unfold_kernel, members, rows), out_shape, "unfold")(place, pair, *messages)


def place_kernel(members, rows, place_ref, *refs):
    for k in range(members):
        for part in range(2):
            refs[-1][block_span(members, rows, part, place_ref[0] ^ k), :] = refs[k][part]


def place_rows(place, pieces):
    members = len(pieces)
    rows, width = pieces[0].shape[1:]
    out_shape = jax.ShapeDtypeStruct((2 * members * rows, width), bf16)
    return call(functools.partial(place_kernel, members, rows), out_shape, "place_rows")(place, *pieces)


def two_products(left, grad_ref, right_ref):
    mixed_left = jnp.dot(left, grad_ref[...], preferred_element_type=f32).astype(bf16)
    return jnp.dot(mixed_left, right_ref[...], preferred_element_type=f32).astype(bf16)


def product_kernel(members, rows, place_ref, *refs):
    grad_pieces = refs[: 2 * members]
    right_ref, left_ref, precond_ref, grad_ref, square_ref = refs[2 * members :]
    for part in range(2):
        for k in range(members):
            grad_ref[block_span(members, rows, part, place_ref[0] ^ k), :] = grad_pieces[part * members + k][...]
    precond = two_products(left_ref[...], grad_ref, right_ref)
    precond_ref[...] = precond
    precond_wide = precond.astype(f32)
    square_ref[...] = jnp.full(square_ref.shape, jnp.sum(precond_wide * precond_wide))


def product(place, grad_pieces, right_full, left_pair):
    members = len(grad_pieces) // 2
    rows, width = grad_pieces[0].shape
    out_shape = (
        jax.ShapeDtypeStruct((2 * rows, width), bf16),
        jax.ShapeDtypeStruct((2 * rows * members, width), bf16),
        jax.ShapeDtypeStruct((8, 128), f32),
    )
    kernel = functools.partial(product_kernel, members, rows)
    return call(kernel, out_shape, "product", 8 * rows * width * width)(place, *grad_pieces, right_full, left_pair)


def per_device(devices, groups, grad_partial, left_stat, right_stat, left_root, right_root, second_moment):
    bits = bits_of(devices)
    top = bits - 1
    members = devices // 2
    index = lax.axis_index("dp")
    member, half = index % members, index // members
    rows, width = left_stat.shape[1:]

    def swap(array, bit):
        return lax.ppermute(array, "dp", [(i, i ^ (1 << bit)) for i in range(devices)])

    def after(array, *arrays):
        return lax.optimization_barrier((array, *arrays))[0]

    def gather_pieces(own, *before_forward):
        pieces = {0: own}
        for bit in range(top - 1, -1, -1):
            for k in list(pieces):
                source = after(pieces[k], *before_forward) if k and before_forward else pieces[k]
                pieces[k ^ (1 << bit)] = swap(source, bit)
        return pieces

    def gather_direct(own):
        pieces = {0: own}
        for k in range(members - 1, 0, -1):
            pieces[k] = lax.ppermute(own, "dp", [(i, i ^ k) for i in range(devices)])
        return pieces

    def by_half(own, partner):
        return jnp.stack([jnp.where(half == 0, own, partner), jnp.where(half == 0, partner, own)])

    def choose(stack, place):
        return lax.dynamic_index_in_dim(stack, place, 0, keepdims=False)

    member_axes = list(range(top - 1, -1, -1))
    grads = grad_partial[0].reshape(2, 2, members, rows, width)
    lower = list(range(top))
    orders = (lower + [top], lower[::-1] + [top])
    first_sends = cut(grads, bits, [order[0] for order in orders], True)
    first_own = cut(after(grads, *first_sends), bits, [order[0] for order in orders], False)
    terms, places = [[], []], [{}, {}]
    right_partner = swap(choose(right_root, 1 - half), top)

    place = jnp.stack([member, half, index])

    def reduce_step(part, step, *arrays):
        bit = orders[part][step]
        if step == 0:
            send = first_sends[part]
        else:
            if arrays:
                array, axes = terms[part][-1]
                terms[part][-1] = (after(array, *arrays), axes)
            send = sum_pieces(place, terms[part], {**places[part], bit: True})
        places[part][bit] = False
        axes = [b for b in [top] + member_axes if b not in places[part]]
        if step == 0:
            terms[part] = [(first_own[part], axes)]
        terms[part].append((swap(send, bit), axes))
        return send

    def reduced(part):
        return sum_pieces(place, terms[part], places[part])

    reduce_step(1, 0)
    reduce_step(0, 0)
    left_partner = swap(after(choose(left_root, 1 - half), terms[0][-1][0], terms[1][-1][0]), top)
    for step in range(1, bits - 1):
        reduce_step(0, step, right_partner, reduce_step(1, step, right_partner))
    round_ends = [t[-1][0] for t in terms]

    halved = members == 4 and rows % 128 == 0

    def pair_rows(own, partner):
        if halved:
            return pack(place, own, partner, members)
        pair = by_half(choose(own, half), partner)
        return pair, pair

    def whole_matrix(pair, pieces):
        if halved:
            return unfold(place, pair, [pieces[k] for k in range(1, members)], members)
        return place_rows(place, [pieces[k] for k in range(members)])

    def exchanged(pieces):
        return [pieces[1 << bit] for bit in member_axes]

    last_send = reduce_step(0, bits - 1, *round_ends, left_partner)
    right_pair, right_message = pair_rows(right_root, right_partner)
    right_pieces = gather_pieces(after(right_message, last_send))
    low = [reduced(0)]
    reduce_step(1, bits - 1, low[0])
    grad_pieces = [gather_pieces(after(low[0], *exchanged(right_pieces)))]
    right_full = whole_matrix(right_pair, right_pieces)
    low.append(after(reduced(1), *exchanged(grad_pieces[0])))
    grad_pieces.append(gather_direct(low[1]))
    own_low = jnp.stack(low)
    theirs = swap(choose(own_low, 1 - half), top)

    span = 2 * rows
    left_pair = by_half(choose(left_root, half), left_partner)
    precond, grad_low, precond_part = product(
        place,
        [pieces[k] for pieces in grad_pieces for k in range(members)],
        right_full,
        left_pair.reshape(span, width),
    )
    precond = precond.reshape(2, rows, width)
    theirs, own_low, grad_low = (after(array, precond) for array in (theirs, own_low, grad_low))

    first_pieces = {0: precond}
    for bit in range(top - 1, 0, -1):
        for k in list(first_pieces):
            first_pieces[k ^ (1 << bit)] = swap(first_pieces[k], bit)
    first_pieces[1] = swap(precond, 0)
    partner = swap(precond, top)

    grad_rows = by_half(choose(own_low, half), theirs).astype(f32)
    moment_new = moment_decay * second_moment + (1.0 - moment_decay) * grad_rows * grad_rows
    adam_dir = grad_rows / (jnp.sqrt(moment_new) + epsilon)
    adam_part = jnp.sum(adam_dir * adam_dir)

    lane = lax.broadcasted_iota(jnp.int32, (8, 128), 1)
    sums = jnp.where(lane == 0, adam_part, precond_part)
    for bit in range(bits_of(groups)):
        sums = sums + lax.ppermute(sums, "blk", [(i, i ^ (1 << bit)) for i in range(groups)])
    for bit in range(bits):
        if bit == top:
            sums = after(sums, partner, *first_pieces.values())
        sums = sums + swap(sums, bit)

    def columns(part):
        return lax.dynamic_slice_in_dim(grad_low, part * members * rows + member * rows, rows, 1)

    contract_rows = (((0,), (0,)), ((), ()))
    contract_cols = (((1,), (1,)), ((), ()))
    right_gram = [lax.dot_general(columns(p), grad_low, contract_rows, preferred_element_type=f32) for p in range(2)]
    right_gram = jnp.stack(right_gram)
    left_gram = lax.dot_general(own_low.reshape(span, width), grad_low, contract_cols, preferred_element_type=f32)
    left_gram = left_gram.reshape(2, rows, width)
    left_away = choose(left_gram, 1 - half).astype(bf16)
    right_away = choose(right_gram, 1 - half).astype(bf16)

    partner, *arrived = lax.optimization_barrier((partner, *first_pieces.values()))
    first_pieces = dict(zip(first_pieces, arrived))
    onward = [k for k in first_pieces if k > 1]
    neighbour = swap(jnp.stack([first_pieces[k] for k in onward] + [partner]), 0)
    for i, k in enumerate(onward):
        first_pieces[k ^ 1] = neighbour[i]
    second_pieces = {0: partner, 1: neighbour[-1]}
    for k in range(members - 1, 1, -1):
        second_pieces[k] = lax.ppermute(partner, "dp", [(i, i ^ k) for i in range(devices)])
    grams_away = after(jnp.stack([left_away, right_away]), partner)
    grams_partner = swap(grams_away, top)

    factor = jnp.sqrt(sums[0, 0] / sums[0, 1])
    update = jnp.zeros((2, 2, members, rows, width), bf16)
    for block, pieces in ((half, first_pieces), (1 - half, second_pieces)):
        for k, piece in pieces.items():
            scaled = (factor * piece.astype(f32)).astype(bf16)
            update = lax.dynamic_update_slice(update, scaled[None, :, None], (block, 0, member ^ k, 0, 0))
    update = update.reshape(2, width, width)
    own_rows = [
        stat_decay * choose(stat, half) + (1.0 - stat_decay) * choose(gram, half)
        for stat, gram in ((left_stat, left_gram), (right_stat, right_gram))
    ]
    left_new, right_new = lax.optimization_barrier(
        tuple(
            lax.dynamic_update_slice(stat, rows_new[None], (half, 0, 0))
            for stat, rows_new in zip((left_stat, right_stat), own_rows)
        )
    )
    left_partner, right_partner = after(grams_partner, update)

    def finish(new, stat, partner):
        rows_new = stat_decay * choose(stat, 1 - half) + (1.0 - stat_decay) * partner.astype(f32)
        return lax.dynamic_update_slice(new, rows_new[None], (1 - half, 0, 0))

    left_new = finish(left_new, left_stat, left_partner)
    right_new = finish(right_new, right_stat, right_partner)
    return (update, left_new, right_new, moment_new)


def solution(mesh):
    in_specs = (
        P("dp", "blk", None, None),
        P("blk", "dp", None),
        P("blk", "dp", None),
        P("blk", "dp", None),
        P("blk", "dp", None),
        P("blk", "dp", None),
    )
    out_specs = (
        P("blk", None, None),
        P("blk", "dp", None),
        P("blk", "dp", None),
        P("blk", "dp", None),
    )

    def body(*arrays):
        return per_device(mesh.shape["dp"], mesh.shape["blk"], *arrays)

    return jax.shard_map(body, mesh=mesh, in_specs=in_specs, out_specs=out_specs, check_vma=False)
```

```python
import functools

import jax
import jax.numpy as jnp
from jax import lax
from jax.experimental import pallas as pl
from jax.experimental.pallas import tpu as pltpu
from jax.sharding import PartitionSpec as P

stat_decay = 0.95
moment_decay = 0.999
epsilon = 1e-08

f32 = jnp.float32
bf16 = jnp.bfloat16


def bits_of(count):
    bits = count.bit_length() - 1
    assert count == 1 << bits
    return bits


VMEM = pl.BlockSpec(memory_space=pltpu.VMEM)
SMEM = pl.BlockSpec(memory_space=pltpu.SMEM)


def call(kernel, out_shape, name, flops=0):
    def run(place, *arrays):
        size = sum(a.size * a.dtype.itemsize for a in arrays)
        return pl.pallas_call(
            kernel,
            out_shape=out_shape,
            in_specs=[SMEM] + [VMEM] * len(arrays),
            out_specs=jax.tree.map(lambda _: VMEM, out_shape),
            compiler_params=pltpu.CompilerParams(vmem_limit_bytes=24 * 2**20),
            cost_estimate=pl.CostEstimate(flops=flops, bytes_accessed=size, transcendentals=0),
            name=name,
        )(place, *arrays)

    return run


def block_span(members, rows, part, member):
    return pl.ds(pl.multiple_of((part * members + member) * rows, rows), rows)


def cut_kernel(bits, orders, flip, grads_ref, *refs):
    out_refs, sems = refs[:-1], refs[-1]
    index = lax.axis_index("dp")
    copies = []
    for part, (first, out_ref) in enumerate(zip(orders, out_refs)):
        own = (index >> first) & 1
        for i in range(out_ref.shape[0]):
            rest = [(i >> j) & 1 for j in range(bits - 1)]
            rest.insert(first, 1 - own if flip else own)
            member = sum(bit << j for j, bit in enumerate(rest[:-1]))
            source = grads_ref.at[rest[-1], part, member]
            copy = pltpu.make_async_copy(source, out_ref.at[i], sems.at[len(copies)])
            copy.start()
            copies.append(copy)
    for copy in copies:
        copy.wait()


def cut(grads, bits, orders, flip):
    members, rows, width = grads.shape[2:]
    shape = jax.ShapeDtypeStruct((members, rows, width), bf16)
    return pl.pallas_call(
        functools.partial(cut_kernel, bits, orders, flip),
        out_shape=(shape, shape),
        in_specs=[pl.BlockSpec(memory_space=pl.ANY)],
        out_specs=(VMEM, VMEM),
        scratch_shapes=[pltpu.SemaphoreType.DMA((2 * members,))],
        compiler_params=pltpu.CompilerParams(vmem_limit_bytes=(56 if flip else 24) * 2**20),
        cost_estimate=pl.CostEstimate(flops=0, bytes_accessed=8 * members * rows * width, transcendentals=0),
        name="cut",
    )(grads)


def sum_kernel(axes_lists, places, free, place_ref, *refs):
    index, out_ref = place_ref[2], refs[-1]
    for i in range(1 << len(free)):
        total = None
        for axes, ref in zip(axes_lists, refs):
            at = 0
            for axis in axes:
                if axis in places:
                    bit = (index >> axis) & 1
                    at = at * 2 + (1 - bit if places[axis] else bit)
                else:
                    at = at * 2 + ((i >> (len(free) - 1 - free.index(axis))) & 1)
            piece = ref[at].astype(f32)
            total = piece if total is None else total + piece
        out_ref[i] = total.astype(bf16)


def sum_pieces(place, terms, places):
    arrays = [array.reshape((-1,) + array.shape[-2:]) for array, _ in terms]
    axes_lists = [axes for _, axes in terms]
    free = [axis for axis in axes_lists[0] if axis not in places]
    shape = arrays[0].shape[-2:]
    kernel = functools.partial(sum_kernel, axes_lists, places, free)
    out = call(kernel, jax.ShapeDtypeStruct((1 << len(free),) + shape, bf16), "sum_pieces")(place, *arrays)
    return out.reshape([2] * len(free) + list(shape))


def neighbour_of(member):
    return member ^ (1 + ((member ^ (member >> 1)) & 1))


def pack_kernel(members, rows, place_ref, own_ref, partner_ref, pair_ref, message_ref):
    member, half = place_ref[0], place_ref[1]
    pair_ref[half] = own_ref[half]
    pair_ref[1 - half] = partner_ref[...]
    role = member >> 1
    blocks = [(0, 0, member), (0, 1, member), (1, 1, member)]
    blocks += [(row_part, part, neighbour_of(member)) for row_part in range(2) for part in range(2)]
    blocks += [(0, role, member ^ 3), (role, 1, member ^ 3)]
    for i, (row_part, part, column) in enumerate(blocks):
        message_ref[i] = pair_ref[row_part, :, block_span(members, rows, part, column)]


def pack(place, own, partner, members):
    rows, width = own.shape[1:]
    out_shape = (jax.ShapeDtypeStruct((2, rows, width), bf16), jax.ShapeDtypeStruct((9, rows, rows), bf16))
    return call(functools.partial(pack_kernel, members, rows), out_shape, "pack")(place, own, partner)


def unfold_kernel(members, rows, place_ref, pair_ref, *refs):
    message_refs, whole_ref = refs[:-1], refs[-1]
    member = place_ref[0]

    def put(row_part, row_member, part, column_member, block):
        whole_ref[
            block_span(members, rows, row_part, row_member), block_span(members, rows, part, column_member)
        ] = block

    for row_part in range(2):
        whole_ref[block_span(members, rows, row_part, member), :] = pair_ref[row_part]
    for k, message_ref in enumerate(message_refs, 1):
        sender = member ^ k
        neighbour, opposite, role = neighbour_of(sender), sender ^ 3, sender >> 1
        for row_part in range(2):
            for part in range(2):
                mine = pair_ref[row_part, :, block_span(members, rows, part, sender)]
                put(part, sender, row_part, member, mine.T)
                block = message_ref[3 + 2 * row_part + part]
                put(row_part, sender, part, neighbour, block)
                put(part, neighbour, row_part, sender, block.T)
        put(0, sender, 0, sender, message_ref[0])
        put(0, sender, 1, sender, message_ref[1])
        put(1, sender, 0, sender, message_ref[1].T)
        put(1, sender, 1, sender, message_ref[2])
        put(0, sender, role, opposite, message_ref[7])
        put(role, opposite, 0, sender, message_ref[7].T)
        put(role, sender, 1, opposite, message_ref[8])
        put(1, opposite, role, sender, message_ref[8].T)


def unfold(place, pair, messages, members):
    rows, width = pair.shape[1:]
    out_shape = jax.ShapeDtypeStruct((2 * members * rows, width), bf16)
    return call(functools.partial(unfold_kernel, members, rows), out_shape, "unfold")(place, pair, *messages)


def place_kernel(members, rows, place_ref, *refs):
    for k in range(members):
        for part in range(2):
            refs[-1][block_span(members, rows, part, place_ref[0] ^ k), :] = refs[k][part]


def place_rows(place, pieces):
    members = len(pieces)
    rows, width = pieces[0].shape[1:]
    out_shape = jax.ShapeDtypeStruct((2 * members * rows, width), bf16)
    return call(functools.partial(place_kernel, members, rows), out_shape, "place_rows")(place, *pieces)


def two_products(left, grad_ref, right_ref):
    mixed_left = jnp.dot(left, grad_ref[...], preferred_element_type=f32).astype(bf16)
    return jnp.dot(mixed_left, right_ref[...], preferred_element_type=f32).astype(bf16)


def product_kernel(members, rows, place_ref, *refs):
    grad_pieces = refs[: 2 * members]
    right_ref, left_ref, precond_ref, grad_ref, square_ref = refs[2 * members :]
    for part in range(2):
        for k in range(members):
            grad_ref[block_span(members, rows, part, place_ref[0] ^ k), :] = grad_pieces[part * members + k][...]
    precond = two_products(left_ref[...], grad_ref, right_ref)
    precond_ref[...] = precond
    precond_wide = precond.astype(f32)
    square_ref[...] = jnp.full(square_ref.shape, jnp.sum(precond_wide * precond_wide))


def product(place, grad_pieces, right_full, left_pair):
    members = len(grad_pieces) // 2
    rows, width = grad_pieces[0].shape
    out_shape = (
        jax.ShapeDtypeStruct((2 * rows, width), bf16),
        jax.ShapeDtypeStruct((2 * rows * members, width), bf16),
        jax.ShapeDtypeStruct((8, 128), f32),
    )
    kernel = functools.partial(product_kernel, members, rows)
    return call(kernel, out_shape, "product", 8 * rows * width * width)(place, *grad_pieces, right_full, left_pair)


def per_device(devices, groups, grad_partial, left_stat, right_stat, left_root, right_root, second_moment):
    bits = bits_of(devices)
    top = bits - 1
    members = devices // 2
    index = lax.axis_index("dp")
    member, half = index % members, index // members
    rows, width = left_stat.shape[1:]

    def swap(array, bit):
        return lax.ppermute(array, "dp", [(i, i ^ (1 << bit)) for i in range(devices)])

    def after(array, *arrays):
        return lax.optimization_barrier((array, *arrays))[0]

    def gather_pieces(own, *before_forward):
        pieces = {0: own}
        for bit in range(top - 1, -1, -1):
            for k in list(pieces):
                source = after(pieces[k], *before_forward) if k and before_forward else pieces[k]
                pieces[k ^ (1 << bit)] = swap(source, bit)
        return pieces

    def gather_direct(own):
        pieces = {0: own}
        for k in range(members - 1, 0, -1):
            pieces[k] = lax.ppermute(own, "dp", [(i, i ^ k) for i in range(devices)])
        return pieces

    def by_half(own, partner):
        return jnp.stack([jnp.where(half == 0, own, partner), jnp.where(half == 0, partner, own)])

    def choose(stack, place):
        return lax.dynamic_index_in_dim(stack, place, 0, keepdims=False)

    member_axes = list(range(top - 1, -1, -1))
    grads = grad_partial[0].reshape(2, 2, members, rows, width)
    lower = list(range(top))
    orders = (lower + [top], lower[::-1] + [top])
    first_sends = cut(grads, bits, [order[0] for order in orders], True)
    first_own = cut(after(grads, *first_sends), bits, [order[0] for order in orders], False)
    terms, places = [[], []], [{}, {}]
    right_partner = swap(choose(right_root, 1 - half), top)

    place = jnp.stack([member, half, index])

    def reduce_step(part, step, *arrays):
        bit = orders[part][step]
        if step == 0:
            send = first_sends[part]
        else:
            if arrays:
                array, axes = terms[part][-1]
                terms[part][-1] = (after(array, *arrays), axes)
            send = sum_pieces(place, terms[part], {**places[part], bit: True})
        places[part][bit] = False
        axes = [b for b in [top] + member_axes if b not in places[part]]
        if step == 0:
            terms[part] = [(first_own[part], axes)]
        terms[part].append((swap(send, bit), axes))
        return send

    def reduced(part):
        return sum_pieces(place, terms[part], places[part])

    reduce_step(1, 0)
    reduce_step(0, 0)
    left_partner = swap(after(choose(left_root, 1 - half), terms[0][-1][0], terms[1][-1][0]), top)
    for step in range(1, bits - 1):
        for part in range(2):
            reduce_step(part, step, right_partner)
    round_ends = [t[-1][0] for t in terms]

    halved = members == 4 and rows % 128 == 0

    def pair_rows(own, partner):
        if halved:
            return pack(place, own, partner, members)
        pair = by_half(choose(own, half), partner)
        return pair, pair

    def whole_matrix(pair, pieces):
        if halved:
            return unfold(place, pair, [pieces[k] for k in range(1, members)], members)
        return place_rows(place, [pieces[k] for k in range(members)])

    def exchanged(pieces):
        return [pieces[1 << bit] for bit in member_axes]

    last_send = reduce_step(0, bits - 1, *round_ends, left_partner)
    right_pair, right_message = pair_rows(right_root, right_partner)
    right_pieces = gather_pieces(after(right_message, last_send))
    low = [reduced(0)]
    reduce_step(1, bits - 1, low[0])
    grad_pieces = [gather_pieces(after(low[0], *exchanged(right_pieces)))]
    right_full = whole_matrix(right_pair, right_pieces)
    low.append(after(reduced(1), *exchanged(grad_pieces[0])))
    grad_pieces.append(gather_direct(low[1]))
    own_low = jnp.stack(low)
    theirs = swap(choose(own_low, 1 - half), top)

    span = 2 * rows
    left_pair = by_half(choose(left_root, half), left_partner)
    precond, grad_low, precond_part = product(
        place,
        [pieces[k] for pieces in grad_pieces for k in range(members)],
        right_full,
        left_pair.reshape(span, width),
    )
    precond = precond.reshape(2, rows, width)
    theirs, own_low, grad_low = (after(array, precond) for array in (theirs, own_low, grad_low))

    first_pieces = {0: precond}
    for bit in range(top - 1, 0, -1):
        for k in list(first_pieces):
            first_pieces[k ^ (1 << bit)] = swap(first_pieces[k], bit)
    first_pieces[1] = swap(precond, 0)
    partner = swap(precond, top)

    grad_rows = by_half(choose(own_low, half), theirs).astype(f32)
    moment_new = moment_decay * second_moment + (1.0 - moment_decay) * grad_rows * grad_rows
    adam_dir = grad_rows / (jnp.sqrt(moment_new) + epsilon)
    adam_part = jnp.sum(adam_dir * adam_dir)

    lane = lax.broadcasted_iota(jnp.int32, (8, 128), 1)
    sums = jnp.where(lane == 0, adam_part, precond_part)
    for bit in range(bits_of(groups)):
        sums = sums + lax.ppermute(sums, "blk", [(i, i ^ (1 << bit)) for i in range(groups)])
    for bit in range(bits):
        if bit == top:
            sums = after(sums, partner, *first_pieces.values())
        sums = sums + swap(sums, bit)

    def columns(part):
        return lax.dynamic_slice_in_dim(grad_low, part * members * rows + member * rows, rows, 1)

    contract_rows = (((0,), (0,)), ((), ()))
    contract_cols = (((1,), (1,)), ((), ()))
    right_gram = [lax.dot_general(columns(p), grad_low, contract_rows, preferred_element_type=f32) for p in range(2)]
    right_gram = jnp.stack(right_gram)
    left_gram = lax.dot_general(own_low.reshape(span, width), grad_low, contract_cols, preferred_element_type=f32)
    left_gram = left_gram.reshape(2, rows, width)
    left_away = choose(left_gram, 1 - half).astype(bf16)
    right_away = choose(right_gram, 1 - half).astype(bf16)

    partner, *arrived = lax.optimization_barrier((partner, *first_pieces.values()))
    first_pieces = dict(zip(first_pieces, arrived))
    onward = [k for k in first_pieces if k > 1]
    neighbour = swap(jnp.stack([first_pieces[k] for k in onward] + [partner]), 0)
    for i, k in enumerate(onward):
        first_pieces[k ^ 1] = neighbour[i]
    second_pieces = {0: partner, 1: neighbour[-1]}
    for k in range(members - 1, 1, -1):
        second_pieces[k] = lax.ppermute(partner, "dp", [(i, i ^ k) for i in range(devices)])
    grams_away = after(jnp.stack([left_away, right_away]), partner)
    grams_partner = swap(grams_away, top)

    factor = jnp.sqrt(sums[0, 0] / sums[0, 1])
    update = jnp.zeros((2, 2, members, rows, width), bf16)
    for block, pieces in ((half, first_pieces), (1 - half, second_pieces)):
        for k, piece in pieces.items():
            scaled = (factor * piece.astype(f32)).astype(bf16)
            update = lax.dynamic_update_slice(update, scaled[None, :, None], (block, 0, member ^ k, 0, 0))
    update = update.reshape(2, width, width)
    own_rows = [
        stat_decay * choose(stat, half) + (1.0 - stat_decay) * choose(gram, half)
        for stat, gram in ((left_stat, left_gram), (right_stat, right_gram))
    ]
    left_new, right_new = lax.optimization_barrier(
        tuple(
            lax.dynamic_update_slice(stat, rows_new[None], (half, 0, 0))
            for stat, rows_new in zip((left_stat, right_stat), own_rows)
        )
    )
    left_partner, right_partner = after(grams_partner, update)

    def finish(new, stat, partner):
        rows_new = stat_decay * choose(stat, 1 - half) + (1.0 - stat_decay) * partner.astype(f32)
        return lax.dynamic_update_slice(new, rows_new[None], (1 - half, 0, 0))

    left_new = finish(left_new, left_stat, left_partner)
    right_new = finish(right_new, right_stat, right_partner)
    return (update, left_new, right_new, moment_new)


def solution(mesh):
    in_specs = (
        P("dp", "blk", None, None),
        P("blk", "dp", None),
        P("blk", "dp", None),
        P("blk", "dp", None),
        P("blk", "dp", None),
        P("blk", "dp", None),
    )
    out_specs = (
        P("blk", None, None),
        P("blk", "dp", None),
        P("blk", "dp", None),
        P("blk", "dp", None),
    )

    def body(*arrays):
        return per_device(mesh.shape["dp"], mesh.shape["blk"], *arrays)

    return jax.shard_map(body, mesh=mesh, in_specs=in_specs, out_specs=out_specs, check_vma=False)
```

```python
import functools

import jax
import jax.numpy as jnp
from jax import lax
from jax.experimental import pallas as pl
from jax.experimental.pallas import tpu as pltpu
from jax.sharding import PartitionSpec as P

stat_decay = 0.95
moment_decay = 0.999
epsilon = 1e-08

f32 = jnp.float32
bf16 = jnp.bfloat16


def bits_of(count):
    bits = count.bit_length() - 1
    assert count == 1 << bits
    return bits


VMEM = pl.BlockSpec(memory_space=pltpu.VMEM)
SMEM = pl.BlockSpec(memory_space=pltpu.SMEM)


def call(kernel, out_shape, name, flops=0, grant=8):
    def run(place, *arrays):
        size = sum(a.size * a.dtype.itemsize for a in arrays)
        return pl.pallas_call(
            kernel,
            out_shape=out_shape,
            in_specs=[SMEM] + [VMEM] * len(arrays),
            out_specs=jax.tree.map(lambda _: VMEM, out_shape),
            compiler_params=pltpu.CompilerParams(vmem_limit_bytes=grant * 2**20),
            cost_estimate=pl.CostEstimate(flops=flops, bytes_accessed=size, transcendentals=0),
            name=name,
        )(place, *arrays)

    return run


def block_span(members, rows, part, member):
    return pl.ds(pl.multiple_of((part * members + member) * rows, rows), rows)


def cut_kernel(bits, orders, flip, grads_ref, *refs):
    out_refs, sems = refs[:-1], refs[-1]
    index = lax.axis_index("dp")
    copies = []
    for part, (first, out_ref) in enumerate(zip(orders, out_refs)):
        own = (index >> first) & 1
        for i in range(out_ref.shape[0]):
            rest = [(i >> j) & 1 for j in range(bits - 1)]
            rest.insert(first, 1 - own if flip else own)
            member = sum(bit << j for j, bit in enumerate(rest[:-1]))
            source = grads_ref.at[rest[-1], part, member]
            copy = pltpu.make_async_copy(source, out_ref.at[i], sems.at[len(copies)])
            copy.start()
            copies.append(copy)
    for copy in copies:
        copy.wait()


def cut(grads, bits, orders, flip):
    members, rows, width = grads.shape[2:]
    shape = jax.ShapeDtypeStruct((members, rows, width), bf16)
    return pl.pallas_call(
        functools.partial(cut_kernel, bits, orders, flip),
        out_shape=(shape, shape),
        in_specs=[pl.BlockSpec(memory_space=pl.ANY)],
        out_specs=(VMEM, VMEM),
        scratch_shapes=[pltpu.SemaphoreType.DMA((2 * members,))],
        compiler_params=pltpu.CompilerParams(vmem_limit_bytes=(56 if flip else 16) * 2**20),
        cost_estimate=pl.CostEstimate(flops=0, bytes_accessed=8 * members * rows * width, transcendentals=0),
        name="cut",
    )(grads)


def sum_kernel(axes_lists, places, free, place_ref, *refs):
    index, out_ref = place_ref[2], refs[-1]
    for i in range(1 << len(free)):
        total = None
        for axes, ref in zip(axes_lists, refs):
            at = 0
            for axis in axes:
                if axis in places:
                    bit = (index >> axis) & 1
                    at = at * 2 + (1 - bit if places[axis] else bit)
                else:
                    at = at * 2 + ((i >> (len(free) - 1 - free.index(axis))) & 1)
            piece = ref[at].astype(f32)
            total = piece if total is None else total + piece
        out_ref[i] = total.astype(bf16)


def sum_pieces(place, terms, places):
    arrays = [array.reshape((-1,) + array.shape[-2:]) for array, _ in terms]
    axes_lists = [axes for _, axes in terms]
    free = [axis for axis in axes_lists[0] if axis not in places]
    shape = arrays[0].shape[-2:]
    kernel = functools.partial(sum_kernel, axes_lists, places, free)
    out = call(kernel, jax.ShapeDtypeStruct((1 << len(free),) + shape, bf16), "sum_pieces")(place, *arrays)
    return out.reshape([2] * len(free) + list(shape))


def neighbour_of(member):
    return member ^ (1 + ((member ^ (member >> 1)) & 1))


def pack_kernel(members, rows, place_ref, own_ref, partner_ref, pair_ref, message_ref):
    member, half = place_ref[0], place_ref[1]
    pair_ref[half] = own_ref[half]
    pair_ref[1 - half] = partner_ref[...]
    role = member >> 1
    blocks = [(0, 0, member), (0, 1, member), (1, 1, member)]
    blocks += [(row_part, part, neighbour_of(member)) for row_part in range(2) for part in range(2)]
    blocks += [(0, role, member ^ 3), (role, 1, member ^ 3)]
    for i, (row_part, part, column) in enumerate(blocks):
        message_ref[i] = pair_ref[row_part, :, block_span(members, rows, part, column)]


def pack(place, own, partner, members):
    rows, width = own.shape[1:]
    out_shape = (jax.ShapeDtypeStruct((2, rows, width), bf16), jax.ShapeDtypeStruct((9, rows, rows), bf16))
    return call(functools.partial(pack_kernel, members, rows), out_shape, "pack")(place, own, partner)


def unfold_kernel(members, rows, place_ref, pair_ref, *refs):
    message_refs, whole_ref = refs[:-1], refs[-1]
    member = place_ref[0]

    def put(row_part, row_member, part, column_member, block):
        whole_ref[
            block_span(members, rows, row_part, row_member), block_span(members, rows, part, column_member)
        ] = block

    for row_part in range(2):
        whole_ref[block_span(members, rows, row_part, member), :] = pair_ref[row_part]
    for k, message_ref in enumerate(message_refs, 1):
        sender = member ^ k
        neighbour, opposite, role = neighbour_of(sender), sender ^ 3, sender >> 1
        for row_part in range(2):
            for part in range(2):
                mine = pair_ref[row_part, :, block_span(members, rows, part, sender)]
                put(part, sender, row_part, member, mine.T)
                block = message_ref[3 + 2 * row_part + part]
                put(row_part, sender, part, neighbour, block)
                put(part, neighbour, row_part, sender, block.T)
        put(0, sender, 0, sender, message_ref[0])
        put(0, sender, 1, sender, message_ref[1])
        put(1, sender, 0, sender, message_ref[1].T)
        put(1, sender, 1, sender, message_ref[2])
        put(0, sender, role, opposite, message_ref[7])
        put(role, opposite, 0, sender, message_ref[7].T)
        put(role, sender, 1, opposite, message_ref[8])
        put(1, opposite, role, sender, message_ref[8].T)


def unfold(place, pair, messages, members):
    rows, width = pair.shape[1:]
    out_shape = jax.ShapeDtypeStruct((2 * members * rows, width), bf16)
    return call(functools.partial(unfold_kernel, members, rows), out_shape, "unfold")(place, pair, *messages)


def place_kernel(members, rows, place_ref, *refs):
    for k in range(members):
        for part in range(2):
            refs[-1][block_span(members, rows, part, place_ref[0] ^ k), :] = refs[k][part]


def place_rows(place, pieces):
    members = len(pieces)
    rows, width = pieces[0].shape[1:]
    out_shape = jax.ShapeDtypeStruct((2 * members * rows, width), bf16)
    return call(functools.partial(place_kernel, members, rows), out_shape, "place_rows")(place, *pieces)


def two_products(left, grad_ref, right_ref):
    mixed_left = jnp.dot(left, grad_ref[...], preferred_element_type=f32).astype(bf16)
    return jnp.dot(mixed_left, right_ref[...], preferred_element_type=f32).astype(bf16)


def product_kernel(members, rows, place_ref, *refs):
    grad_pieces = refs[: 2 * members]
    right_ref, left_ref, precond_ref, grad_ref, square_ref = refs[2 * members :]
    for part in range(2):
        for k in range(members):
            grad_ref[block_span(members, rows, part, place_ref[0] ^ k), :] = grad_pieces[part * members + k][...]
    precond = two_products(left_ref[...], grad_ref, right_ref)
    precond_ref[...] = precond
    precond_wide = precond.astype(f32)
    square_ref[...] = jnp.full(square_ref.shape, jnp.sum(precond_wide * precond_wide))


def product(place, grad_pieces, right_full, left_pair):
    members = len(grad_pieces) // 2
    rows, width = grad_pieces[0].shape
    out_shape = (
        jax.ShapeDtypeStruct((2 * rows, width), bf16),
        jax.ShapeDtypeStruct((2 * rows * members, width), bf16),
        jax.ShapeDtypeStruct((8, 128), f32),
    )
    kernel = functools.partial(product_kernel, members, rows)
    return call(kernel, out_shape, "product", 8 * rows * width * width, 16)(place, *grad_pieces, right_full, left_pair)


def per_device(devices, groups, grad_partial, left_stat, right_stat, left_root, right_root, second_moment):
    bits = bits_of(devices)
    top = bits - 1
    members = devices // 2
    index = lax.axis_index("dp")
    member, half = index % members, index // members
    rows, width = left_stat.shape[1:]

    def swap(array, bit):
        return lax.ppermute(array, "dp", [(i, i ^ (1 << bit)) for i in range(devices)])

    def after(array, *arrays):
        return lax.optimization_barrier((array, *arrays))[0]

    def gather_pieces(own, *before_forward):
        pieces = {0: own}
        for bit in range(top - 1, -1, -1):
            for k in list(pieces):
                source = after(pieces[k], *before_forward) if k and before_forward else pieces[k]
                pieces[k ^ (1 << bit)] = swap(source, bit)
        return pieces

    def gather_direct(own):
        pieces = {0: own}
        for k in range(members - 1, 0, -1):
            pieces[k] = lax.ppermute(own, "dp", [(i, i ^ k) for i in range(devices)])
        return pieces

    def by_half(own, partner):
        return jnp.stack([jnp.where(half == 0, own, partner), jnp.where(half == 0, partner, own)])

    def choose(stack, place):
        return lax.dynamic_index_in_dim(stack, place, 0, keepdims=False)

    member_axes = list(range(top - 1, -1, -1))
    grads = grad_partial[0].reshape(2, 2, members, rows, width)
    lower = list(range(top))
    orders = (lower + [top], lower[::-1] + [top])
    first_sends = cut(grads, bits, [order[0] for order in orders], True)
    first_own = cut(after(grads, *first_sends), bits, [order[0] for order in orders], False)
    terms, places = [[], []], [{}, {}]
    right_partner = swap(choose(right_root, 1 - half), top)

    place = jnp.stack([member, half, index])

    def reduce_step(part, step, *arrays):
        bit = orders[part][step]
        if step == 0:
            send = first_sends[part]
        else:
            if arrays:
                array, axes = terms[part][-1]
                terms[part][-1] = (after(array, *arrays), axes)
            send = sum_pieces(place, terms[part], {**places[part], bit: True})
        places[part][bit] = False
        axes = [b for b in [top] + member_axes if b not in places[part]]
        if step == 0:
            terms[part] = [(first_own[part], axes)]
        terms[part].append((swap(send, bit), axes))
        return send

    def reduced(part):
        return sum_pieces(place, terms[part], places[part])

    reduce_step(1, 0)
    reduce_step(0, 0)
    left_partner = swap(after(choose(left_root, 1 - half), terms[0][-1][0], terms[1][-1][0]), top)
    for step in range(1, bits - 1):
        for part in range(2):
            reduce_step(part, step, right_partner)
    round_ends = [t[-1][0] for t in terms]

    halved = members == 4 and rows % 128 == 0

    def pair_rows(own, partner):
        if halved:
            return pack(place, own, partner, members)
        pair = by_half(choose(own, half), partner)
        return pair, pair

    def whole_matrix(pair, pieces):
        if halved:
            return unfold(place, pair, [pieces[k] for k in range(1, members)], members)
        return place_rows(place, [pieces[k] for k in range(members)])

    def exchanged(pieces):
        return [pieces[1 << bit] for bit in member_axes]

    last_send = reduce_step(0, bits - 1, *round_ends, left_partner)
    right_pair, right_message = pair_rows(right_root, right_partner)
    right_pieces = gather_pieces(after(right_message, last_send))
    low = [reduced(0)]
    reduce_step(1, bits - 1, low[0])
    grad_pieces = [gather_pieces(after(low[0], *exchanged(right_pieces)))]
    right_full = whole_matrix(right_pair, right_pieces)
    low.append(after(reduced(1), *exchanged(grad_pieces[0])))
    grad_pieces.append(gather_direct(low[1]))
    own_low = jnp.stack(low)
    theirs = swap(choose(own_low, 1 - half), top)

    span = 2 * rows
    left_pair = by_half(choose(left_root, half), left_partner)
    precond, grad_low, precond_part = product(
        place,
        [pieces[k] for pieces in grad_pieces for k in range(members)],
        right_full,
        left_pair.reshape(span, width),
    )
    precond = precond.reshape(2, rows, width)
    theirs, own_low, grad_low = (after(array, precond) for array in (theirs, own_low, grad_low))

    first_pieces = {0: precond}
    for bit in range(top - 1, 0, -1):
        for k in list(first_pieces):
            first_pieces[k ^ (1 << bit)] = swap(first_pieces[k], bit)
    first_pieces[1] = swap(precond, 0)
    partner = swap(precond, top)

    grad_rows = by_half(choose(own_low, half), theirs).astype(f32)
    moment_new = moment_decay * second_moment + (1.0 - moment_decay) * grad_rows * grad_rows
    adam_dir = grad_rows / (jnp.sqrt(moment_new) + epsilon)
    adam_part = jnp.sum(adam_dir * adam_dir)

    lane = lax.broadcasted_iota(jnp.int32, (8, 128), 1)
    sums = jnp.where(lane == 0, adam_part, precond_part)
    for bit in range(bits_of(groups)):
        sums = sums + lax.ppermute(sums, "blk", [(i, i ^ (1 << bit)) for i in range(groups)])
    for bit in range(bits):
        if bit == top:
            sums = after(sums, partner, *first_pieces.values())
        sums = sums + swap(sums, bit)

    def columns(part):
        return lax.dynamic_slice_in_dim(grad_low, part * members * rows + member * rows, rows, 1)

    contract_rows = (((0,), (0,)), ((), ()))
    contract_cols = (((1,), (1,)), ((), ()))
    right_gram = [lax.dot_general(columns(p), grad_low, contract_rows, preferred_element_type=f32) for p in range(2)]
    right_gram = jnp.stack(right_gram)
    left_gram = lax.dot_general(own_low.reshape(span, width), grad_low, contract_cols, preferred_element_type=f32)
    left_gram = left_gram.reshape(2, rows, width)
    left_away = choose(left_gram, 1 - half).astype(bf16)
    right_away = choose(right_gram, 1 - half).astype(bf16)

    partner, *arrived = lax.optimization_barrier((partner, *first_pieces.values()))
    first_pieces = dict(zip(first_pieces, arrived))
    onward = [k for k in first_pieces if k > 1]
    neighbour = swap(jnp.stack([first_pieces[k] for k in onward] + [partner]), 0)
    for i, k in enumerate(onward):
        first_pieces[k ^ 1] = neighbour[i]
    second_pieces = {0: partner, 1: neighbour[-1]}
    for k in range(members - 1, 1, -1):
        second_pieces[k] = lax.ppermute(partner, "dp", [(i, i ^ k) for i in range(devices)])
    grams_away = after(jnp.stack([left_away, right_away]), partner)
    grams_partner = swap(grams_away, top)

    factor = jnp.sqrt(sums[0, 0] / sums[0, 1])
    update = jnp.zeros((2, 2, members, rows, width), bf16)
    for block, pieces in ((half, first_pieces), (1 - half, second_pieces)):
        for k, piece in pieces.items():
            scaled = (factor * piece.astype(f32)).astype(bf16)
            update = lax.dynamic_update_slice(update, scaled[None, :, None], (block, 0, member ^ k, 0, 0))
    update = update.reshape(2, width, width)
    own_rows = [
        stat_decay * choose(stat, half) + (1.0 - stat_decay) * choose(gram, half)
        for stat, gram in ((left_stat, left_gram), (right_stat, right_gram))
    ]
    left_new, right_new = lax.optimization_barrier(
        tuple(
            lax.dynamic_update_slice(stat, rows_new[None], (half, 0, 0))
            for stat, rows_new in zip((left_stat, right_stat), own_rows)
        )
    )
    left_partner, right_partner = after(grams_partner, update)

    def finish(new, stat, partner):
        rows_new = stat_decay * choose(stat, 1 - half) + (1.0 - stat_decay) * partner.astype(f32)
        return lax.dynamic_update_slice(new, rows_new[None], (1 - half, 0, 0))

    left_new = finish(left_new, left_stat, left_partner)
    right_new = finish(right_new, right_stat, right_partner)
    return (update, left_new, right_new, moment_new)


def solution(mesh):
    in_specs = (
        P("dp", "blk", None, None),
        P("blk", "dp", None),
        P("blk", "dp", None),
        P("blk", "dp", None),
        P("blk", "dp", None),
        P("blk", "dp", None),
    )
    out_specs = (
        P("blk", None, None),
        P("blk", "dp", None),
        P("blk", "dp", None),
        P("blk", "dp", None),
    )

    def body(*arrays):
        return per_device(mesh.shape["dp"], mesh.shape["blk"], *arrays)

    return jax.shard_map(body, mesh=mesh, in_specs=in_specs, out_specs=out_specs, check_vma=False)
```

```python
import functools

import jax
import jax.numpy as jnp
from jax import lax
from jax.experimental import pallas as pl
from jax.experimental.pallas import tpu as pltpu
from jax.sharding import PartitionSpec as P

stat_decay = 0.95
moment_decay = 0.999
epsilon = 1e-08

f32 = jnp.float32
bf16 = jnp.bfloat16


def bits_of(count):
    bits = count.bit_length() - 1
    assert count == 1 << bits
    return bits


VMEM = pl.BlockSpec(memory_space=pltpu.VMEM)
SMEM = pl.BlockSpec(memory_space=pltpu.SMEM)


def call(kernel, out_shape, name, flops=0):
    def run(place, *arrays):
        size = sum(a.size * a.dtype.itemsize for a in arrays)
        return pl.pallas_call(
            kernel,
            out_shape=out_shape,
            in_specs=[SMEM] + [VMEM] * len(arrays),
            out_specs=jax.tree.map(lambda _: VMEM, out_shape),
            compiler_params=pltpu.CompilerParams(vmem_limit_bytes=24 * 2**20),
            cost_estimate=pl.CostEstimate(flops=flops, bytes_accessed=size, transcendentals=0),
            name=name,
        )(place, *arrays)

    return run


def block_span(members, rows, part, member):
    return pl.ds(pl.multiple_of((part * members + member) * rows, rows), rows)


def cut_kernel(bits, orders, flip, grads_ref, *refs):
    out_refs, sems = refs[:-1], refs[-1]
    index = lax.axis_index("dp")
    copies = []
    for part, (first, out_ref) in enumerate(zip(orders, out_refs)):
        own = (index >> first) & 1
        for i in range(out_ref.shape[0]):
            rest = [(i >> j) & 1 for j in range(bits - 1)]
            rest.insert(first, 1 - own if flip else own)
            member = sum(bit << j for j, bit in enumerate(rest[:-1]))
            source = grads_ref.at[rest[-1], part, member]
            copy = pltpu.make_async_copy(source, out_ref.at[i], sems.at[len(copies)])
            copy.start()
            copies.append(copy)
    for copy in copies:
        copy.wait()


def cut(grads, bits, orders, flip):
    members, rows, width = grads.shape[2:]
    shape = jax.ShapeDtypeStruct((members, rows, width), bf16)
    return pl.pallas_call(
        functools.partial(cut_kernel, bits, orders, flip),
        out_shape=(shape, shape),
        in_specs=[pl.BlockSpec(memory_space=pl.ANY)],
        out_specs=(VMEM, VMEM),
        scratch_shapes=[pltpu.SemaphoreType.DMA((2 * members,))],
        compiler_params=pltpu.CompilerParams(vmem_limit_bytes=(56 if flip else 24) * 2**20),
        cost_estimate=pl.CostEstimate(flops=0, bytes_accessed=8 * members * rows * width, transcendentals=0),
        name="cut",
    )(grads)


def sum_kernel(axes_lists, places, free, place_ref, *refs):
    index, out_ref = place_ref[2], refs[-1]
    for i in range(1 << len(free)):
        total = None
        for axes, ref in zip(axes_lists, refs):
            at = 0
            for axis in axes:
                if axis in places:
                    bit = (index >> axis) & 1
                    at = at * 2 + (1 - bit if places[axis] else bit)
                else:
                    at = at * 2 + ((i >> (len(free) - 1 - free.index(axis))) & 1)
            piece = ref[at].astype(f32)
            total = piece if total is None else total + piece
        out_ref[i] = total.astype(bf16)


def sum_pieces(place, terms, places):
    arrays = [array.reshape((-1,) + array.shape[-2:]) for array, _ in terms]
    axes_lists = [axes for _, axes in terms]
    free = [axis for axis in axes_lists[0] if axis not in places]
    shape = arrays[0].shape[-2:]
    kernel = functools.partial(sum_kernel, axes_lists, places, free)
    out_shape = jax.ShapeDtypeStruct((1 << len(free),) + shape, bf16)
    out = call(kernel, out_shape, "sum_pieces", 1 << 30)(place, *arrays)
    return out.reshape([2] * len(free) + list(shape))


def neighbour_of(member):
    return member ^ (1 + ((member ^ (member >> 1)) & 1))


def pack_kernel(members, rows, place_ref, own_ref, partner_ref, pair_ref, message_ref):
    member, half = place_ref[0], place_ref[1]
    pair_ref[half] = own_ref[half]
    pair_ref[1 - half] = partner_ref[...]
    role = member >> 1
    blocks = [(0, 0, member), (0, 1, member), (1, 1, member)]
    blocks += [(row_part, part, neighbour_of(member)) for row_part in range(2) for part in range(2)]
    blocks += [(0, role, member ^ 3), (role, 1, member ^ 3)]
    for i, (row_part, part, column) in enumerate(blocks):
        message_ref[i] = pair_ref[row_part, :, block_span(members, rows, part, column)]


def pack(place, own, partner, members):
    rows, width = own.shape[1:]
    out_shape = (jax.ShapeDtypeStruct((2, rows, width), bf16), jax.ShapeDtypeStruct((9, rows, rows), bf16))
    return call(functools.partial(pack_kernel, members, rows), out_shape, "pack")(place, own, partner)


def unfold_kernel(members, rows, place_ref, pair_ref, *refs):
    message_refs, whole_ref = refs[:-1], refs[-1]
    member = place_ref[0]

    def put(row_part, row_member, part, column_member, block):
        whole_ref[
            block_span(members, rows, row_part, row_member), block_span(members, rows, part, column_member)
        ] = block

    for row_part in range(2):
        whole_ref[block_span(members, rows, row_part, member), :] = pair_ref[row_part]
    for k, message_ref in enumerate(message_refs, 1):
        sender = member ^ k
        neighbour, opposite, role = neighbour_of(sender), sender ^ 3, sender >> 1
        for row_part in range(2):
            for part in range(2):
                mine = pair_ref[row_part, :, block_span(members, rows, part, sender)]
                put(part, sender, row_part, member, mine.T)
                block = message_ref[3 + 2 * row_part + part]
                put(row_part, sender, part, neighbour, block)
                put(part, neighbour, row_part, sender, block.T)
        put(0, sender, 0, sender, message_ref[0])
        put(0, sender, 1, sender, message_ref[1])
        put(1, sender, 0, sender, message_ref[1].T)
        put(1, sender, 1, sender, message_ref[2])
        put(0, sender, role, opposite, message_ref[7])
        put(role, opposite, 0, sender, message_ref[7].T)
        put(role, sender, 1, opposite, message_ref[8])
        put(1, opposite, role, sender, message_ref[8].T)


def unfold(place, pair, messages, members):
    rows, width = pair.shape[1:]
    out_shape = jax.ShapeDtypeStruct((2 * members * rows, width), bf16)
    return call(functools.partial(unfold_kernel, members, rows), out_shape, "unfold")(place, pair, *messages)


def place_kernel(members, rows, place_ref, *refs):
    for k in range(members):
        for part in range(2):
            refs[-1][block_span(members, rows, part, place_ref[0] ^ k), :] = refs[k][part]


def place_rows(place, pieces):
    members = len(pieces)
    rows, width = pieces[0].shape[1:]
    out_shape = jax.ShapeDtypeStruct((2 * members * rows, width), bf16)
    return call(functools.partial(place_kernel, members, rows), out_shape, "place_rows")(place, *pieces)


def two_products(left, grad_ref, right_ref):
    mixed_left = jnp.dot(left, grad_ref[...], preferred_element_type=f32).astype(bf16)
    return jnp.dot(mixed_left, right_ref[...], preferred_element_type=f32).astype(bf16)


def product_kernel(members, rows, place_ref, *refs):
    grad_pieces = refs[: 2 * members]
    right_ref, left_ref, precond_ref, grad_ref, square_ref = refs[2 * members :]
    for part in range(2):
        for k in range(members):
            grad_ref[block_span(members, rows, part, place_ref[0] ^ k), :] = grad_pieces[part * members + k][...]
    precond = two_products(left_ref[...], grad_ref, right_ref)
    precond_ref[...] = precond
    precond_wide = precond.astype(f32)
    square_ref[...] = jnp.full(square_ref.shape, jnp.sum(precond_wide * precond_wide))


def product(place, grad_pieces, right_full, left_pair):
    members = len(grad_pieces) // 2
    rows, width = grad_pieces[0].shape
    out_shape = (
        jax.ShapeDtypeStruct((2 * rows, width), bf16),
        jax.ShapeDtypeStruct((2 * rows * members, width), bf16),
        jax.ShapeDtypeStruct((8, 128), f32),
    )
    kernel = functools.partial(product_kernel, members, rows)
    return call(kernel, out_shape, "product", 8 * rows * width * width)(place, *grad_pieces, right_full, left_pair)


def per_device(devices, groups, grad_partial, left_stat, right_stat, left_root, right_root, second_moment):
    bits = bits_of(devices)
    top = bits - 1
    members = devices // 2
    index = lax.axis_index("dp")
    member, half = index % members, index // members
    rows, width = left_stat.shape[1:]

    def swap(array, bit):
        return lax.ppermute(array, "dp", [(i, i ^ (1 << bit)) for i in range(devices)])

    def after(array, *arrays):
        return lax.optimization_barrier((array, *arrays))[0]

    def gather_pieces(own, *before_forward):
        pieces = {0: own}
        for bit in range(top - 1, -1, -1):
            for k in list(pieces):
                source = after(pieces[k], *before_forward) if k and before_forward else pieces[k]
                pieces[k ^ (1 << bit)] = swap(source, bit)
        return pieces

    def gather_direct(own):
        pieces = {0: own}
        for k in range(members - 1, 0, -1):
            pieces[k] = lax.ppermute(own, "dp", [(i, i ^ k) for i in range(devices)])
        return pieces

    def by_half(own, partner):
        return jnp.stack([jnp.where(half == 0, own, partner), jnp.where(half == 0, partner, own)])

    def choose(stack, place):
        return lax.dynamic_index_in_dim(stack, place, 0, keepdims=False)

    member_axes = list(range(top - 1, -1, -1))
    grads = grad_partial[0].reshape(2, 2, members, rows, width)
    lower = list(range(top))
    orders = (lower + [top], lower[::-1] + [top])
    first_sends = cut(grads, bits, [order[0] for order in orders], True)
    first_own = cut(after(grads, *first_sends), bits, [order[0] for order in orders], False)
    terms, places = [[], []], [{}, {}]
    right_partner = swap(choose(right_root, 1 - half), top)

    place = jnp.stack([member, half, index])

    def reduce_step(part, step, *arrays):
        bit = orders[part][step]
        if step == 0:
            send = first_sends[part]
        else:
            if arrays:
                array, axes = terms[part][-1]
                terms[part][-1] = (after(array, *arrays), axes)
            send = sum_pieces(place, terms[part], {**places[part], bit: True})
        places[part][bit] = False
        axes = [b for b in [top] + member_axes if b not in places[part]]
        if step == 0:
            terms[part] = [(first_own[part], axes)]
        terms[part].append((swap(send, bit), axes))
        return send

    def reduced(part):
        return sum_pieces(place, terms[part], places[part])

    halved = members == 4 and rows % 128 == 0

    def pair_rows(own, partner):
        if halved:
            return pack(place, own, partner, members)
        pair = by_half(choose(own, half), partner)
        return pair, pair

    def whole_matrix(pair, pieces):
        if halved:
            return unfold(place, pair, [pieces[k] for k in range(1, members)], members)
        return place_rows(place, [pieces[k] for k in range(members)])

    def exchanged(pieces):
        return [pieces[1 << bit] for bit in member_axes]

    right_pair, right_message = pair_rows(right_root, right_partner)
    reduce_step(1, 0)
    reduce_step(0, 0)
    left_partner = swap(after(choose(left_root, 1 - half), terms[0][-1][0], terms[1][-1][0]), top)
    for step in range(1, bits - 1):
        for part in range(2):
            reduce_step(part, step, right_message)
    round_ends = [t[-1][0] for t in terms]

    last_send = reduce_step(0, bits - 1, *round_ends, left_partner)
    right_pieces = gather_pieces(after(right_message, last_send))
    low = [reduced(0)]
    reduce_step(1, bits - 1, low[0])
    grad_pieces = [gather_pieces(after(low[0], *exchanged(right_pieces)))]
    right_full = whole_matrix(right_pair, right_pieces)
    low.append(after(reduced(1), *exchanged(grad_pieces[0])))
    grad_pieces.append(gather_direct(low[1]))
    own_low = jnp.stack(low)
    theirs = swap(choose(own_low, 1 - half), top)

    span = 2 * rows
    left_pair = by_half(choose(left_root, half), left_partner)
    precond, grad_low, precond_part = product(
        place,
        [pieces[k] for pieces in grad_pieces for k in range(members)],
        right_full,
        left_pair.reshape(span, width),
    )
    precond = precond.reshape(2, rows, width)
    theirs, own_low, grad_low = (after(array, precond) for array in (theirs, own_low, grad_low))

    first_pieces = {0: precond}
    for bit in range(top - 1, 0, -1):
        for k in list(first_pieces):
            first_pieces[k ^ (1 << bit)] = swap(first_pieces[k], bit)
    first_pieces[1] = swap(precond, 0)
    partner = swap(precond, top)

    grad_rows = by_half(choose(own_low, half), theirs).astype(f32)
    moment_new = moment_decay * second_moment + (1.0 - moment_decay) * grad_rows * grad_rows
    adam_dir = grad_rows / (jnp.sqrt(moment_new) + epsilon)
    adam_part = jnp.sum(adam_dir * adam_dir)

    lane = lax.broadcasted_iota(jnp.int32, (8, 128), 1)
    sums = jnp.where(lane == 0, adam_part, precond_part)
    for bit in range(bits_of(groups)):
        sums = sums + lax.ppermute(sums, "blk", [(i, i ^ (1 << bit)) for i in range(groups)])
    for bit in range(bits):
        if bit == top:
            sums = after(sums, partner, *first_pieces.values())
        sums = sums + swap(sums, bit)

    def columns(part):
        return lax.dynamic_slice_in_dim(grad_low, part * members * rows + member * rows, rows, 1)

    contract_rows = (((0,), (0,)), ((), ()))
    contract_cols = (((1,), (1,)), ((), ()))
    right_gram = [lax.dot_general(columns(p), grad_low, contract_rows, preferred_element_type=f32) for p in range(2)]
    right_gram = jnp.stack(right_gram)
    left_gram = lax.dot_general(own_low.reshape(span, width), grad_low, contract_cols, preferred_element_type=f32)
    left_gram = left_gram.reshape(2, rows, width)
    left_away = choose(left_gram, 1 - half).astype(bf16)
    right_away = choose(right_gram, 1 - half).astype(bf16)

    partner, *arrived = lax.optimization_barrier((partner, *first_pieces.values()))
    first_pieces = dict(zip(first_pieces, arrived))
    onward = [k for k in first_pieces if k > 1]
    neighbour = swap(jnp.stack([first_pieces[k] for k in onward] + [partner]), 0)
    for i, k in enumerate(onward):
        first_pieces[k ^ 1] = neighbour[i]
    second_pieces = {0: partner, 1: neighbour[-1]}
    for k in range(members - 1, 1, -1):
        second_pieces[k] = lax.ppermute(partner, "dp", [(i, i ^ k) for i in range(devices)])
    grams_away = after(jnp.stack([left_away, right_away]), partner)
    grams_partner = swap(grams_away, top)

    factor = jnp.sqrt(sums[0, 0] / sums[0, 1])
    update = jnp.zeros((2, 2, members, rows, width), bf16)
    for block, pieces in ((half, first_pieces), (1 - half, second_pieces)):
        for k, piece in pieces.items():
            scaled = (factor * piece.astype(f32)).astype(bf16)
            update = lax.dynamic_update_slice(update, scaled[None, :, None], (block, 0, member ^ k, 0, 0))
    update = update.reshape(2, width, width)
    own_rows = [
        stat_decay * choose(stat, half) + (1.0 - stat_decay) * choose(gram, half)
        for stat, gram in ((left_stat, left_gram), (right_stat, right_gram))
    ]
    left_new, right_new = lax.optimization_barrier(
        tuple(
            lax.dynamic_update_slice(stat, rows_new[None], (half, 0, 0))
            for stat, rows_new in zip((left_stat, right_stat), own_rows)
        )
    )
    left_partner, right_partner = after(grams_partner, update)

    def finish(new, stat, partner):
        rows_new = stat_decay * choose(stat, 1 - half) + (1.0 - stat_decay) * partner.astype(f32)
        return lax.dynamic_update_slice(new, rows_new[None], (1 - half, 0, 0))

    left_new = finish(left_new, left_stat, left_partner)
    right_new = finish(right_new, right_stat, right_partner)
    return (update, left_new, right_new, moment_new)


def solution(mesh):
    in_specs = (
        P("dp", "blk", None, None),
        P("blk", "dp", None),
        P("blk", "dp", None),
        P("blk", "dp", None),
        P("blk", "dp", None),
        P("blk", "dp", None),
    )
    out_specs = (
        P("blk", None, None),
        P("blk", "dp", None),
        P("blk", "dp", None),
        P("blk", "dp", None),
    )

    def body(*arrays):
        return per_device(mesh.shape["dp"], mesh.shape["blk"], *arrays)

    return jax.shard_map(body, mesh=mesh, in_specs=in_specs, out_specs=out_specs, check_vma=False)
```

```python
import functools

import jax
import jax.numpy as jnp
from jax import lax
from jax.experimental import pallas as pl
from jax.experimental.pallas import tpu as pltpu
from jax.sharding import PartitionSpec as P

stat_decay = 0.95
moment_decay = 0.999
epsilon = 1e-08

f32 = jnp.float32
bf16 = jnp.bfloat16


def bits_of(count):
    bits = count.bit_length() - 1
    assert count == 1 << bits
    return bits


VMEM = pl.BlockSpec(memory_space=pltpu.VMEM)
SMEM = pl.BlockSpec(memory_space=pltpu.SMEM)


def call(kernel, out_shape, name, flops=0):
    def run(place, *arrays):
        size = sum(a.size * a.dtype.itemsize for a in arrays)
        return pl.pallas_call(
            kernel,
            out_shape=out_shape,
            in_specs=[SMEM] + [VMEM] * len(arrays),
            out_specs=jax.tree.map(lambda _: VMEM, out_shape),
            compiler_params=pltpu.CompilerParams(vmem_limit_bytes=24 * 2**20),
            cost_estimate=pl.CostEstimate(flops=flops, bytes_accessed=size, transcendentals=0),
            name=name,
        )(place, *arrays)

    return run


def block_span(members, rows, part, member):
    return pl.ds(pl.multiple_of((part * members + member) * rows, rows), rows)


def cut_kernel(bits, orders, flip, grads_ref, *refs):
    out_refs, sems = refs[:-1], refs[-1]
    index = lax.axis_index("dp")
    copies = []
    for part, (first, out_ref) in enumerate(zip(orders, out_refs)):
        own = (index >> first) & 1
        for i in range(out_ref.shape[0]):
            rest = [(i >> j) & 1 for j in range(bits - 1)]
            rest.insert(first, 1 - own if flip else own)
            member = sum(bit << j for j, bit in enumerate(rest[:-1]))
            source = grads_ref.at[rest[-1], part, member]
            copy = pltpu.make_async_copy(source, out_ref.at[i], sems.at[len(copies)])
            copy.start()
            copies.append(copy)
    for copy in copies:
        copy.wait()


def cut(grads, bits, orders, flip):
    members, rows, width = grads.shape[2:]
    shape = jax.ShapeDtypeStruct((members, rows, width), bf16)
    return pl.pallas_call(
        functools.partial(cut_kernel, bits, orders, flip),
        out_shape=(shape, shape),
        in_specs=[pl.BlockSpec(memory_space=pl.ANY)],
        out_specs=(VMEM, VMEM),
        scratch_shapes=[pltpu.SemaphoreType.DMA((2 * members,))],
        compiler_params=pltpu.CompilerParams(vmem_limit_bytes=(56 if flip else 24) * 2**20),
        cost_estimate=pl.CostEstimate(flops=0, bytes_accessed=8 * members * rows * width, transcendentals=0),
        name="cut",
    )(grads)


def sum_kernel(axes_lists, places, free, place_ref, *refs):
    index, out_ref = place_ref[2], refs[-1]
    for i in range(1 << len(free)):
        total = None
        for axes, ref in zip(axes_lists, refs):
            at = 0
            for axis in axes:
                if axis in places:
                    bit = (index >> axis) & 1
                    at = at * 2 + (1 - bit if places[axis] else bit)
                else:
                    at = at * 2 + ((i >> (len(free) - 1 - free.index(axis))) & 1)
            piece = ref[at].astype(f32)
            total = piece if total is None else total + piece
        out_ref[i] = total.astype(bf16)


def sum_pieces(place, terms, places):
    arrays = [array.reshape((-1,) + array.shape[-2:]) for array, _ in terms]
    axes_lists = [axes for _, axes in terms]
    free = [axis for axis in axes_lists[0] if axis not in places]
    shape = arrays[0].shape[-2:]
    kernel = functools.partial(sum_kernel, axes_lists, places, free)
    out = call(kernel, jax.ShapeDtypeStruct((1 << len(free),) + shape, bf16), "sum_pieces")(place, *arrays)
    return out.reshape([2] * len(free) + list(shape))


def neighbour_of(member):
    return member ^ (1 + ((member ^ (member >> 1)) & 1))


def pack_kernel(members, rows, place_ref, own_ref, partner_ref, pair_ref, message_ref):
    member, half = place_ref[0], place_ref[1]
    pair_ref[half] = own_ref[half]
    pair_ref[1 - half] = partner_ref[...]
    role = member >> 1
    blocks = [(0, 0, member), (0, 1, member), (1, 1, member)]
    blocks += [(row_part, part, neighbour_of(member)) for row_part in range(2) for part in range(2)]
    blocks += [(0, role, member ^ 3), (role, 1, member ^ 3)]
    for i, (row_part, part, column) in enumerate(blocks):
        message_ref[i] = pair_ref[row_part, :, block_span(members, rows, part, column)]


def pack(place, own, partner, members):
    rows, width = own.shape[1:]
    out_shape = (jax.ShapeDtypeStruct((2, rows, width), bf16), jax.ShapeDtypeStruct((9, rows, rows), bf16))
    return call(functools.partial(pack_kernel, members, rows), out_shape, "pack")(place, own, partner)


def unfold_kernel(members, rows, place_ref, pair_ref, *refs):
    message_refs, whole_ref = refs[:-1], refs[-1]
    member = place_ref[0]

    def put(row_part, row_member, part, column_member, block):
        whole_ref[
            block_span(members, rows, row_part, row_member), block_span(members, rows, part, column_member)
        ] = block

    for row_part in range(2):
        whole_ref[block_span(members, rows, row_part, member), :] = pair_ref[row_part]
    for k, message_ref in enumerate(message_refs, 1):
        sender = member ^ k
        neighbour, opposite, role = neighbour_of(sender), sender ^ 3, sender >> 1
        for row_part in range(2):
            for part in range(2):
                mine = pair_ref[row_part, :, block_span(members, rows, part, sender)]
                put(part, sender, row_part, member, mine.T)
                block = message_ref[3 + 2 * row_part + part]
                put(row_part, sender, part, neighbour, block)
                put(part, neighbour, row_part, sender, block.T)
        put(0, sender, 0, sender, message_ref[0])
        put(0, sender, 1, sender, message_ref[1])
        put(1, sender, 0, sender, message_ref[1].T)
        put(1, sender, 1, sender, message_ref[2])
        put(0, sender, role, opposite, message_ref[7])
        put(role, opposite, 0, sender, message_ref[7].T)
        put(role, sender, 1, opposite, message_ref[8])
        put(1, opposite, role, sender, message_ref[8].T)


def unfold(place, pair, messages, members):
    rows, width = pair.shape[1:]
    out_shape = jax.ShapeDtypeStruct((2 * members * rows, width), bf16)
    return call(functools.partial(unfold_kernel, members, rows), out_shape, "unfold")(place, pair, *messages)


def place_kernel(members, rows, place_ref, *refs):
    for k in range(members):
        for part in range(2):
            refs[-1][block_span(members, rows, part, place_ref[0] ^ k), :] = refs[k][part]


def place_rows(place, pieces):
    members = len(pieces)
    rows, width = pieces[0].shape[1:]
    out_shape = jax.ShapeDtypeStruct((2 * members * rows, width), bf16)
    return call(functools.partial(place_kernel, members, rows), out_shape, "place_rows")(place, *pieces)


def two_products(left, grad_ref, right_ref):
    mixed_left = jnp.dot(left, grad_ref[...], preferred_element_type=f32).astype(bf16)
    return jnp.dot(mixed_left, right_ref[...], preferred_element_type=f32).astype(bf16)


def product_kernel(members, rows, place_ref, *refs):
    grad_pieces = refs[: 2 * members]
    right_ref, left_ref, precond_ref, grad_ref, square_ref = refs[2 * members :]
    for part in range(2):
        for k in range(members):
            grad_ref[block_span(members, rows, part, place_ref[0] ^ k), :] = grad_pieces[part * members + k][...]
    precond = two_products(left_ref[...], grad_ref, right_ref)
    precond_ref[...] = precond
    precond_wide = precond.astype(f32)
    square_ref[...] = jnp.full(square_ref.shape, jnp.sum(precond_wide * precond_wide))


def product(place, grad_pieces, right_full, left_pair):
    members = len(grad_pieces) // 2
    rows, width = grad_pieces[0].shape
    out_shape = (
        jax.ShapeDtypeStruct((2 * rows, width), bf16),
        jax.ShapeDtypeStruct((2 * rows * members, width), bf16),
        jax.ShapeDtypeStruct((8, 128), f32),
    )
    kernel = functools.partial(product_kernel, members, rows)
    return call(kernel, out_shape, "product", 8 * rows * width * width)(place, *grad_pieces, right_full, left_pair)


def per_device(devices, groups, grad_partial, left_stat, right_stat, left_root, right_root, second_moment):
    bits = bits_of(devices)
    top = bits - 1
    members = devices // 2
    index = lax.axis_index("dp")
    member, half = index % members, index // members
    rows, width = left_stat.shape[1:]

    def swap(array, bit):
        return lax.ppermute(array, "dp", [(i, i ^ (1 << bit)) for i in range(devices)])

    def after(array, *arrays):
        return lax.optimization_barrier((array, *arrays))[0]

    def gather_pieces(own, *before_forward):
        pieces = {0: own}
        for bit in range(top - 1, -1, -1):
            for k in list(pieces):
                source = after(pieces[k], *before_forward) if k and before_forward else pieces[k]
                pieces[k ^ (1 << bit)] = swap(source, bit)
        return pieces

    def gather_direct(own):
        pieces = {0: own}
        for k in range(members - 1, 0, -1):
            pieces[k] = lax.ppermute(own, "dp", [(i, i ^ k) for i in range(devices)])
        return pieces

    def by_half(own, partner):
        return jnp.stack([jnp.where(half == 0, own, partner), jnp.where(half == 0, partner, own)])

    def choose(stack, place):
        return lax.dynamic_index_in_dim(stack, place, 0, keepdims=False)

    member_axes = list(range(top - 1, -1, -1))
    grads = grad_partial[0].reshape(2, 2, members, rows, width)
    lower = list(range(top))
    orders = (lower + [top], lower[::-1] + [top])
    first_sends = cut(grads, bits, [order[0] for order in orders], True)
    first_own = cut(after(grads, *first_sends), bits, [order[0] for order in orders], False)
    terms, places = [[], []], [{}, {}]
    right_partner = swap(choose(right_root, 1 - half), top)

    place = jnp.stack([member, half, index])

    def reduce_step(part, step, *arrays):
        bit = orders[part][step]
        if step == 0:
            send = first_sends[part]
        else:
            if arrays:
                array, axes = terms[part][-1]
                terms[part][-1] = (after(array, *arrays), axes)
            send = sum_pieces(place, terms[part], {**places[part], bit: True})
        places[part][bit] = False
        axes = [b for b in [top] + member_axes if b not in places[part]]
        if step == 0:
            terms[part] = [(first_own[part], axes)]
        terms[part].append((swap(send, bit), axes))
        return send

    def reduced(part):
        return sum_pieces(place, terms[part], places[part])

    reduce_step(1, 0)
    reduce_step(0, 0)
    left_partner = swap(after(choose(left_root, 1 - half), terms[0][-1][0], terms[1][-1][0]), top)
    for step in range(1, bits - 1):
        for part in range(2):
            reduce_step(part, step, right_partner)
    round_ends = [t[-1][0] for t in terms]

    halved = members == 4 and rows % 128 == 0

    def pair_rows(own, partner):
        if halved:
            return pack(place, own, partner, members)
        pair = by_half(choose(own, half), partner)
        return pair, pair

    def whole_matrix(pair, pieces):
        if halved:
            return unfold(place, pair, [pieces[k] for k in range(1, members)], members)
        return place_rows(place, [pieces[k] for k in range(members)])

    def exchanged(pieces):
        return [pieces[1 << bit] for bit in member_axes]

    last_send = reduce_step(0, bits - 1, *round_ends, left_partner)
    right_pair, right_message = pair_rows(right_root, right_partner)
    right_pieces = gather_pieces(after(right_message, last_send))
    low = [reduced(0)]
    reduce_step(1, bits - 1, low[0])
    grad_pieces = [gather_pieces(after(low[0], *exchanged(right_pieces)))]
    right_full = whole_matrix(right_pair, right_pieces)
    low.append(after(reduced(1), *exchanged(grad_pieces[0])))
    grad_pieces.append(gather_direct(low[1]))
    own_low = jnp.stack(low)
    theirs = swap(choose(own_low, 1 - half), top)

    span = 2 * rows
    left_pair = by_half(choose(left_root, half), left_partner)
    precond, grad_low, precond_part = product(
        place,
        [pieces[k] for pieces in grad_pieces for k in range(members)],
        right_full,
        left_pair.reshape(span, width),
    )
    precond = precond.reshape(2, rows, width)
    theirs, own_low, grad_low = (after(array, precond) for array in (theirs, own_low, grad_low))

    first_pieces = {0: precond}
    for bit in range(top - 1, 0, -1):
        for k in list(first_pieces):
            first_pieces[k ^ (1 << bit)] = swap(first_pieces[k], bit)
    first_pieces[1] = swap(precond, 0)
    partner = swap(precond, top)

    grad_rows = by_half(choose(own_low, half), theirs).astype(f32)
    moment_new = moment_decay * second_moment + (1.0 - moment_decay) * grad_rows * grad_rows
    adam_dir = grad_rows / (jnp.sqrt(moment_new) + epsilon)
    adam_part = jnp.sum(adam_dir * adam_dir)

    lane = lax.broadcasted_iota(jnp.int32, (8, 128), 1)
    sums = jnp.where(lane == 0, adam_part, precond_part)
    for bit in range(bits_of(groups)):
        sums = sums + lax.ppermute(sums, "blk", [(i, i ^ (1 << bit)) for i in range(groups)])
    for bit in (*range(top - 1), top):
        sums = sums + swap(sums, bit)
    sums = after(sums, partner, *first_pieces.values())
    sums = sums + swap(sums, top - 1)

    def columns(part):
        return lax.dynamic_slice_in_dim(grad_low, part * members * rows + member * rows, rows, 1)

    contract_rows = (((0,), (0,)), ((), ()))
    contract_cols = (((1,), (1,)), ((), ()))
    right_gram = [lax.dot_general(columns(p), grad_low, contract_rows, preferred_element_type=f32) for p in range(2)]
    right_gram = jnp.stack(right_gram)
    left_gram = lax.dot_general(own_low.reshape(span, width), grad_low, contract_cols, preferred_element_type=f32)
    left_gram = left_gram.reshape(2, rows, width)
    left_away = choose(left_gram, 1 - half).astype(bf16)
    right_away = choose(right_gram, 1 - half).astype(bf16)

    partner, *arrived = lax.optimization_barrier((partner, *first_pieces.values()))
    first_pieces = dict(zip(first_pieces, arrived))
    onward = [k for k in first_pieces if k > 1]
    neighbour = swap(jnp.stack([first_pieces[k] for k in onward] + [partner]), 0)
    for i, k in enumerate(onward):
        first_pieces[k ^ 1] = neighbour[i]
    second_pieces = {0: partner, 1: neighbour[-1]}
    for k in range(members - 1, 1, -1):
        second_pieces[k] = lax.ppermute(partner, "dp", [(i, i ^ k) for i in range(devices)])
    grams_away = after(jnp.stack([left_away, right_away]), partner)
    grams_partner = swap(grams_away, top)

    factor = jnp.sqrt(sums[0, 0] / sums[0, 1])
    update = jnp.zeros((2, 2, members, rows, width), bf16)
    for block, pieces in ((half, first_pieces), (1 - half, second_pieces)):
        for k, piece in pieces.items():
            scaled = (factor * piece.astype(f32)).astype(bf16)
            update = lax.dynamic_update_slice(update, scaled[None, :, None], (block, 0, member ^ k, 0, 0))
    update = update.reshape(2, width, width)
    own_rows = [
        stat_decay * choose(stat, half) + (1.0 - stat_decay) * choose(gram, half)
        for stat, gram in ((left_stat, left_gram), (right_stat, right_gram))
    ]
    left_new, right_new = lax.optimization_barrier(
        tuple(
            lax.dynamic_update_slice(stat, rows_new[None], (half, 0, 0))
            for stat, rows_new in zip((left_stat, right_stat), own_rows)
        )
    )
    left_partner, right_partner = after(grams_partner, update)

    def finish(new, stat, partner):
        rows_new = stat_decay * choose(stat, 1 - half) + (1.0 - stat_decay) * partner.astype(f32)
        return lax.dynamic_update_slice(new, rows_new[None], (1 - half, 0, 0))

    left_new = finish(left_new, left_stat, left_partner)
    right_new = finish(right_new, right_stat, right_partner)
    return (update, left_new, right_new, moment_new)


def solution(mesh):
    in_specs = (
        P("dp", "blk", None, None),
        P("blk", "dp", None),
        P("blk", "dp", None),
        P("blk", "dp", None),
        P("blk", "dp", None),
        P("blk", "dp", None),
    )
    out_specs = (
        P("blk", None, None),
        P("blk", "dp", None),
        P("blk", "dp", None),
        P("blk", "dp", None),
    )

    def body(*arrays):
        return per_device(mesh.shape["dp"], mesh.shape["blk"], *arrays)

    return jax.shard_map(body, mesh=mesh, in_specs=in_specs, out_specs=out_specs, check_vma=False)
```

```python
import functools

import jax
import jax.numpy as jnp
from jax import lax
from jax.experimental import pallas as pl
from jax.experimental.pallas import tpu as pltpu
from jax.sharding import PartitionSpec as P

stat_decay = 0.95
moment_decay = 0.999
epsilon = 1e-08

f32 = jnp.float32
bf16 = jnp.bfloat16


def bits_of(count):
    bits = count.bit_length() - 1
    assert count == 1 << bits
    return bits


VMEM = pl.BlockSpec(memory_space=pltpu.VMEM)
SMEM = pl.BlockSpec(memory_space=pltpu.SMEM)


def call(kernel, out_shape, name, flops=0):
    def run(place, *arrays):
        size = sum(a.size * a.dtype.itemsize for a in arrays)
        return pl.pallas_call(
            kernel,
            out_shape=out_shape,
            in_specs=[SMEM] + [VMEM] * len(arrays),
            out_specs=jax.tree.map(lambda _: VMEM, out_shape),
            compiler_params=pltpu.CompilerParams(vmem_limit_bytes=24 * 2**20),
            cost_estimate=pl.CostEstimate(flops=flops, bytes_accessed=size, transcendentals=0),
            name=name,
        )(place, *arrays)

    return run


def block_span(members, rows, part, member):
    return pl.ds(pl.multiple_of((part * members + member) * rows, rows), rows)


def cut_kernel(bits, orders, flip, grads_ref, *refs):
    out_refs, sems = refs[:-1], refs[-1]
    index = lax.axis_index("dp")
    copies = []
    for part, (first, out_ref) in enumerate(zip(orders, out_refs)):
        own = (index >> first) & 1
        for i in range(out_ref.shape[0]):
            rest = [(i >> j) & 1 for j in range(bits - 1)]
            rest.insert(first, 1 - own if flip else own)
            member = sum(bit << j for j, bit in enumerate(rest[:-1]))
            source = grads_ref.at[rest[-1], part, member]
            copy = pltpu.make_async_copy(source, out_ref.at[i], sems.at[len(copies)])
            copy.start()
            copies.append(copy)
    for copy in copies:
        copy.wait()


def cut(grads, bits, orders, flip):
    members, rows, width = grads.shape[2:]
    shape = jax.ShapeDtypeStruct((members, rows, width), bf16)
    return pl.pallas_call(
        functools.partial(cut_kernel, bits, orders, flip),
        out_shape=(shape, shape),
        in_specs=[pl.BlockSpec(memory_space=pl.ANY)],
        out_specs=(VMEM, VMEM),
        scratch_shapes=[pltpu.SemaphoreType.DMA((2 * members,))],
        compiler_params=pltpu.CompilerParams(vmem_limit_bytes=(56 if flip else 24) * 2**20),
        cost_estimate=pl.CostEstimate(flops=0, bytes_accessed=8 * members * rows * width, transcendentals=0),
        name="cut",
    )(grads)


def sum_kernel(axes_lists, places, free, place_ref, *refs):
    index, out_ref = place_ref[2], refs[-1]
    for i in range(1 << len(free)):
        total = None
        for axes, ref in zip(axes_lists, refs):
            at = 0
            for axis in axes:
                if axis in places:
                    bit = (index >> axis) & 1
                    at = at * 2 + (1 - bit if places[axis] else bit)
                else:
                    at = at * 2 + ((i >> (len(free) - 1 - free.index(axis))) & 1)
            piece = ref[at].astype(f32)
            total = piece if total is None else total + piece
        out_ref[i] = total.astype(bf16)


def sum_pieces(place, terms, places):
    arrays = [array.reshape((-1,) + array.shape[-2:]) for array, _ in terms]
    axes_lists = [axes for _, axes in terms]
    free = [axis for axis in axes_lists[0] if axis not in places]
    shape = arrays[0].shape[-2:]
    kernel = functools.partial(sum_kernel, axes_lists, places, free)
    out = call(kernel, jax.ShapeDtypeStruct((1 << len(free),) + shape, bf16), "sum_pieces")(place, *arrays)
    return out.reshape([2] * len(free) + list(shape))


def neighbour_of(member):
    return member ^ (1 + ((member ^ (member >> 1)) & 1))


def pack_kernel(members, rows, place_ref, own_ref, partner_ref, pair_ref, message_ref):
    member, half = place_ref[0], place_ref[1]
    pair_ref[half] = own_ref[half]
    pair_ref[1 - half] = partner_ref[...]
    role = member >> 1
    blocks = [(0, 0, member), (0, 1, member), (1, 1, member)]
    blocks += [(row_part, part, neighbour_of(member)) for row_part in range(2) for part in range(2)]
    blocks += [(0, role, member ^ 3), (role, 1, member ^ 3)]
    for i, (row_part, part, column) in enumerate(blocks):
        message_ref[i] = pair_ref[row_part, :, block_span(members, rows, part, column)]


def pack(place, own, partner, members):
    rows, width = own.shape[1:]
    out_shape = (jax.ShapeDtypeStruct((2, rows, width), bf16), jax.ShapeDtypeStruct((9, rows, rows), bf16))
    return call(functools.partial(pack_kernel, members, rows), out_shape, "pack")(place, own, partner)


def unfold_kernel(members, rows, place_ref, pair_ref, *refs):
    message_refs, whole_ref = refs[:-1], refs[-1]
    member = place_ref[0]

    def put(row_part, row_member, part, column_member, block):
        whole_ref[
            block_span(members, rows, row_part, row_member), block_span(members, rows, part, column_member)
        ] = block

    for row_part in range(2):
        whole_ref[block_span(members, rows, row_part, member), :] = pair_ref[row_part]
    for k, message_ref in enumerate(message_refs, 1):
        sender = member ^ k
        neighbour, opposite, role = neighbour_of(sender), sender ^ 3, sender >> 1
        for row_part in range(2):
            for part in range(2):
                mine = pair_ref[row_part, :, block_span(members, rows, part, sender)]
                put(part, sender, row_part, member, mine.T)
                block = message_ref[3 + 2 * row_part + part]
                put(row_part, sender, part, neighbour, block)
                put(part, neighbour, row_part, sender, block.T)
        put(0, sender, 0, sender, message_ref[0])
        put(0, sender, 1, sender, message_ref[1])
        put(1, sender, 0, sender, message_ref[1].T)
        put(1, sender, 1, sender, message_ref[2])
        put(0, sender, role, opposite, message_ref[7])
        put(role, opposite, 0, sender, message_ref[7].T)
        put(role, sender, 1, opposite, message_ref[8])
        put(1, opposite, role, sender, message_ref[8].T)


def unfold(place, pair, messages, members):
    rows, width = pair.shape[1:]
    out_shape = jax.ShapeDtypeStruct((2 * members * rows, width), bf16)
    return call(functools.partial(unfold_kernel, members, rows), out_shape, "unfold")(place, pair, *messages)


def place_kernel(members, rows, place_ref, *refs):
    for k in range(members):
        for part in range(2):
            refs[-1][block_span(members, rows, part, place_ref[0] ^ k), :] = refs[k][part]


def place_rows(place, pieces):
    members = len(pieces)
    rows, width = pieces[0].shape[1:]
    out_shape = jax.ShapeDtypeStruct((2 * members * rows, width), bf16)
    return call(functools.partial(place_kernel, members, rows), out_shape, "place_rows")(place, *pieces)


def two_products(left, grad_ref, right_ref):
    mixed_left = jnp.dot(left, grad_ref[...], preferred_element_type=f32).astype(bf16)
    return jnp.dot(mixed_left, right_ref[...], preferred_element_type=f32).astype(bf16)


def product_kernel(members, rows, place_ref, *refs):
    grad_pieces = refs[: 2 * members]
    right_ref, left_ref, precond_ref, grad_ref, square_ref = refs[2 * members :]
    for part in range(2):
        for k in range(members):
            grad_ref[block_span(members, rows, part, place_ref[0] ^ k), :] = grad_pieces[part * members + k][...]
    precond = two_products(left_ref[...], grad_ref, right_ref)
    precond_ref[...] = precond
    precond_wide = precond.astype(f32)
    square_ref[...] = jnp.full(square_ref.shape, jnp.sum(precond_wide * precond_wide))


def product(place, grad_pieces, right_full, left_pair):
    members = len(grad_pieces) // 2
    rows, width = grad_pieces[0].shape
    out_shape = (
        jax.ShapeDtypeStruct((2 * rows, width), bf16),
        jax.ShapeDtypeStruct((2 * rows * members, width), bf16),
        jax.ShapeDtypeStruct((8, 128), f32),
    )
    kernel = functools.partial(product_kernel, members, rows)
    return call(kernel, out_shape, "product", 8 * rows * width * width)(place, *grad_pieces, right_full, left_pair)


def per_device(devices, groups, grad_partial, left_stat, right_stat, left_root, right_root, second_moment):
    bits = bits_of(devices)
    top = bits - 1
    members = devices // 2
    index = lax.axis_index("dp")
    member, half = index % members, index // members
    rows, width = left_stat.shape[1:]

    def swap(array, bit):
        return lax.ppermute(array, "dp", [(i, i ^ (1 << bit)) for i in range(devices)])

    def after(array, *arrays):
        return lax.optimization_barrier((array, *arrays))[0]

    def gather_pieces(own, *before_forward):
        pieces = {0: own}
        for bit in range(top - 1, -1, -1):
            for k in list(pieces):
                source = after(pieces[k], *before_forward) if k and before_forward else pieces[k]
                pieces[k ^ (1 << bit)] = swap(source, bit)
        return pieces

    def gather_direct(own):
        pieces = {0: own}
        for k in range(members - 1, 0, -1):
            pieces[k] = lax.ppermute(own, "dp", [(i, i ^ k) for i in range(devices)])
        return pieces

    def by_half(own, partner):
        return jnp.stack([jnp.where(half == 0, own, partner), jnp.where(half == 0, partner, own)])

    def choose(stack, place):
        return lax.dynamic_index_in_dim(stack, place, 0, keepdims=False)

    member_axes = list(range(top - 1, -1, -1))
    grads = grad_partial[0].reshape(2, 2, members, rows, width)
    lower = list(range(top))
    orders = (lower + [top], lower[::-1] + [top])
    first_sends = cut(grads, bits, [order[0] for order in orders], True)
    first_own = cut(after(grads, *first_sends), bits, [order[0] for order in orders], False)
    terms, places = [[], []], [{}, {}]
    roots_away = jnp.stack([choose(right_root, 1 - half), choose(left_root, 1 - half)])
    right_partner, left_partner = swap(roots_away, top)

    place = jnp.stack([member, half, index])

    def reduce_step(part, step, *arrays):
        bit = orders[part][step]
        if step == 0:
            send = first_sends[part]
        else:
            if arrays:
                array, axes = terms[part][-1]
                terms[part][-1] = (after(array, *arrays), axes)
            send = sum_pieces(place, terms[part], {**places[part], bit: True})
        places[part][bit] = False
        axes = [b for b in [top] + member_axes if b not in places[part]]
        if step == 0:
            terms[part] = [(first_own[part], axes)]
        terms[part].append((swap(send, bit), axes))
        return send

    def reduced(part):
        return sum_pieces(place, terms[part], places[part])

    reduce_step(1, 0)
    reduce_step(0, 0)
    for step in range(1, bits - 1):
        for part in range(2):
            reduce_step(part, step, right_partner)
    round_ends = [t[-1][0] for t in terms]

    halved = members == 4 and rows % 128 == 0

    def pair_rows(own, partner):
        if halved:
            return pack(place, own, partner, members)
        pair = by_half(choose(own, half), partner)
        return pair, pair

    def whole_matrix(pair, pieces):
        if halved:
            return unfold(place, pair, [pieces[k] for k in range(1, members)], members)
        return place_rows(place, [pieces[k] for k in range(members)])

    def exchanged(pieces):
        return [pieces[1 << bit] for bit in member_axes]

    last_send = reduce_step(0, bits - 1, *round_ends, left_partner)
    right_pair, right_message = pair_rows(right_root, right_partner)
    right_pieces = gather_pieces(after(right_message, last_send))
    low = [reduced(0)]
    reduce_step(1, bits - 1, low[0])
    grad_pieces = [gather_pieces(after(low[0], *exchanged(right_pieces)))]
    right_full = whole_matrix(right_pair, right_pieces)
    low.append(after(reduced(1), *exchanged(grad_pieces[0])))
    grad_pieces.append(gather_direct(low[1]))
    own_low = jnp.stack(low)
    theirs = swap(choose(own_low, 1 - half), top)

    span = 2 * rows
    left_pair = by_half(choose(left_root, half), left_partner)
    precond, grad_low, precond_part = product(
        place,
        [pieces[k] for pieces in grad_pieces for k in range(members)],
        right_full,
        left_pair.reshape(span, width),
    )
    precond = precond.reshape(2, rows, width)
    theirs, own_low, grad_low = (after(array, precond) for array in (theirs, own_low, grad_low))

    first_pieces = {0: precond}
    for bit in range(top - 1, 0, -1):
        for k in list(first_pieces):
            first_pieces[k ^ (1 << bit)] = swap(first_pieces[k], bit)
    first_pieces[1] = swap(precond, 0)
    partner = swap(precond, top)

    grad_rows = by_half(choose(own_low, half), theirs).astype(f32)
    moment_new = moment_decay * second_moment + (1.0 - moment_decay) * grad_rows * grad_rows
    adam_dir = grad_rows / (jnp.sqrt(moment_new) + epsilon)
    adam_part = jnp.sum(adam_dir * adam_dir)

    lane = lax.broadcasted_iota(jnp.int32, (8, 128), 1)
    sums = jnp.where(lane == 0, adam_part, precond_part)
    for bit in range(bits_of(groups)):
        sums = sums + lax.ppermute(sums, "blk", [(i, i ^ (1 << bit)) for i in range(groups)])
    for bit in (*range(top - 1), top):
        sums = sums + swap(sums, bit)
    sums = after(sums, partner, *first_pieces.values())
    sums = sums + swap(sums, top - 1)

    def columns(part):
        return lax.dynamic_slice_in_dim(grad_low, part * members * rows + member * rows, rows, 1)

    contract_rows = (((0,), (0,)), ((), ()))
    contract_cols = (((1,), (1,)), ((), ()))
    right_gram = [lax.dot_general(columns(p), grad_low, contract_rows, preferred_element_type=f32) for p in range(2)]
    right_gram = jnp.stack(right_gram)
    left_gram = lax.dot_general(own_low.reshape(span, width), grad_low, contract_cols, preferred_element_type=f32)
    left_gram = left_gram.reshape(2, rows, width)
    left_away = choose(left_gram, 1 - half).astype(bf16)
    right_away = choose(right_gram, 1 - half).astype(bf16)

    partner, *arrived = lax.optimization_barrier((partner, *first_pieces.values()))
    first_pieces = dict(zip(first_pieces, arrived))
    onward = [k for k in first_pieces if k > 1]
    neighbour = swap(jnp.stack([first_pieces[k] for k in onward] + [partner]), 0)
    for i, k in enumerate(onward):
        first_pieces[k ^ 1] = neighbour[i]
    second_pieces = {0: partner, 1: neighbour[-1]}
    for k in range(members - 1, 1, -1):
        second_pieces[k] = lax.ppermute(partner, "dp", [(i, i ^ k) for i in range(devices)])
    grams_away = after(jnp.stack([left_away, right_away]), partner)
    grams_partner = swap(grams_away, top)

    factor = jnp.sqrt(sums[0, 0] / sums[0, 1])
    update = jnp.zeros((2, 2, members, rows, width), bf16)
    for block, pieces in ((half, first_pieces), (1 - half, second_pieces)):
        for k, piece in pieces.items():
            scaled = (factor * piece.astype(f32)).astype(bf16)
            update = lax.dynamic_update_slice(update, scaled[None, :, None], (block, 0, member ^ k, 0, 0))
    update = update.reshape(2, width, width)
    own_rows = [
        stat_decay * choose(stat, half) + (1.0 - stat_decay) * choose(gram, half)
        for stat, gram in ((left_stat, left_gram), (right_stat, right_gram))
    ]
    left_new, right_new = lax.optimization_barrier(
        tuple(
            lax.dynamic_update_slice(stat, rows_new[None], (half, 0, 0))
            for stat, rows_new in zip((left_stat, right_stat), own_rows)
        )
    )
    left_partner, right_partner = after(grams_partner, update)

    def finish(new, stat, partner):
        rows_new = stat_decay * choose(stat, 1 - half) + (1.0 - stat_decay) * partner.astype(f32)
        return lax.dynamic_update_slice(new, rows_new[None], (1 - half, 0, 0))

    left_new = finish(left_new, left_stat, left_partner)
    right_new = finish(right_new, right_stat, right_partner)
    return (update, left_new, right_new, moment_new)


def solution(mesh):
    in_specs = (
        P("dp", "blk", None, None),
        P("blk", "dp", None),
        P("blk", "dp", None),
        P("blk", "dp", None),
        P("blk", "dp", None),
        P("blk", "dp", None),
    )
    out_specs = (
        P("blk", None, None),
        P("blk", "dp", None),
        P("blk", "dp", None),
        P("blk", "dp", None),
    )

    def body(*arrays):
        return per_device(mesh.shape["dp"], mesh.shape["blk"], *arrays)

    return jax.shard_map(body, mesh=mesh, in_specs=in_specs, out_specs=out_specs, check_vma=False)
```
